32 devices in a mesh: groups: 2 (over y), tensor: 4 (over z), tenant: 2 (over x), dp: 2 (over core).
Axes of the slice: x: 2, y: 2, z: 4, core: 2. Of those that a mesh axis runs over, the one named last changes fastest.
Arguments:
- tokens: bfloat16 [4096, 4096], P(('groups', 'tenant', 'dp'), 'tensor'), parts along dimension 0, may hold values from -6 to 6
- query_weight: bfloat16 [4096, 4096], P(None, 'tensor'), may hold values from -0.125 to 0.125
- adapter_down_maps: bfloat16 [8, 4096, 16], P('tenant', 'tensor'), may hold values from -0.09375 to 0.09375
- adapter_up_maps: bfloat16 [8, 16, 4096], P('tenant', None, 'tensor'), may hold values from -1.5 to 1.5
- tenant_row_counts: int32 [16], P('groups'), parts along dimension 0, may hold values from 1 to 640, as said below
- tenant_adapter_slot: int32 [8], replicated, may hold values from 0 to 7, each once
- query_cotangent: bfloat16 [4096, 4096], P(('groups', 'tenant', 'dp'), 'tensor'), parts along dimension 0, may hold values from -6 to 6
Outputs:
- query: bfloat16 [4096, 4096], P(('groups', 'tenant', 'dp'), 'tensor'), parts along dimension 0
- token_input_gradient: bfloat16 [4096, 4096], P(('groups', 'tenant', 'dp'), 'tensor'), parts along dimension 0
- weight_grad: bfloat16 [8192, 4096], P('groups', 'tensor'), parts along dimension 0
- down_grad: float32 [16, 4096, 16], P(('groups', 'tenant'), 'tensor'), parts along dimension 0
- up_grad: float32 [16, 16, 4096], P(('groups', 'tenant'), None, 'tensor'), parts along dimension 0
The draws below stay inside these ranges and needn't reach their ends.
There are 2 independent parts, one for each index of `groups`. The reference program is written for one: setup_inputs(seed, part) draws one part's arguments, and reference() takes and returns one part's arrays. A program takes and returns all parts, laid end to end along the dimension named above; an argument that names none is the same for every part. Nothing has to cross between parts.
Inputs may be any that keep to these rules, and one draw needn't show every extreme that they name: The sum over tenants of ceil(tenant_row_counts / 128) equals 16; tenants' blocks stand in tenant order from block 0. `tenant_adapter_slot`: each slot is named by exactly one tenant; slot s lies on index s // 4 of tenant.
All inputs are finite; a program needn't handle non-finite values.
Results may differ from the reference program's by a relative error of at most 0.014.
Values may be sent and summed in bfloat16 or wider, within the bound.
No kernel may reach another device: no remote copies, remote signals or barrier semaphores. Data moves between devices by JAX's collectives and lax.ppermute only.
A program may use at most 128 MiB of HBM per device.

```python
import jax
import jax.numpy as jnp
from jax import lax

MODEL_WIDTH = 4096
ADAPTER_RANK = 16
BLOCK_ROWS = 128
TENANT_COUNT = 8
TOKENS = 2048
BLOCKS = 16
N_TENSOR = 4


def draw_tenant_row_counts(key, part):
    key = jax.random.fold_in(key, 11)
    heavy_key, first_key, second_key, tail_key = jax.random.split(key, 4)
    extra = BLOCKS - TENANT_COUNT
    heavy_extra = extra - extra // 2
    spread_extra = extra // 2
    heavy = jax.random.randint(heavy_key, (), 0, TENANT_COUNT)
    first = jax.random.randint(first_key, (spread_extra,), 0, TENANT_COUNT - 1)
    second = jax.random.randint(second_key, (spread_extra,), 0, TENANT_COUNT - 1)
    picked = jnp.minimum(first, second)
    picked = jnp.where(picked >= heavy, picked + 1, picked)
    tenant_ids = jnp.arange(TENANT_COUNT, dtype=jnp.int32)
    hits = (picked[:, None] == tenant_ids[None, :]).astype(jnp.int32)
    heavy_mask = (tenant_ids == heavy).astype(jnp.int32)
    block_count = 1 + jnp.sum(hits, axis=0) + heavy_extra * heavy_mask
    tail_rows = jax.random.randint(tail_key, (TENANT_COUNT,), 1, BLOCK_ROWS + 1)
    tail_rows = jnp.where(tenant_ids == heavy, BLOCK_ROWS, tail_rows)
    tail_rows = jnp.where(tenant_ids == (heavy + 1) % TENANT_COUNT, 1, tail_rows)
    return (BLOCK_ROWS * (block_count - 1) + tail_rows).astype(jnp.int32)


def strengthened(entries, own_key, source, target, shards_of, factor):
    owner, partner = [(jnp.arange(entries.shape[dim]) // (entries.shape[dim] // shards_of)).reshape([-1 if axis == dim else 1 for axis in range(entries.ndim)]) for dim in (source, target)]
    chosen = jax.random.permutation(own_key, shards_of)[partner]
    strong = (owner == chosen) | (owner == (partner + shards_of // 2) % shards_of)
    return jnp.where(strong, factor * entries, entries)


def level_of(key, dims, cuts, low, top_value):
    def one(axis_at, blocks):
        heights = jax.random.uniform(jax.random.fold_in(jax.random.fold_in(key, 6), axis_at), (blocks,), jnp.float32, low / len(cuts), top_value / len(cuts))
        return jnp.repeat(jnp.exp(heights), dims[axis_at] // blocks).reshape((-1,) + (1,) * (len(dims) - axis_at - 1))

    factor_of = one(*cuts[0])
    for cut in cuts[1:]:
        factor_of = factor_of * one(*cut)
    return factor_of


def normal_values(own_key, extent, deviation, most, shards=(), kind=jnp.bfloat16):
    drawn = jax.random.normal(own_key, extent, jnp.float32) * deviation
    if len(shards) > 0:
        drawn = level_of(own_key, extent, shards, -0.22, 0.18) * drawn
    return jnp.clip(drawn, min=-most, max=most).astype(kind)


def heavy_noise(key, shape, deviation, limit, pieces, heavy, kind=jnp.bfloat16):
    values = deviation * jax.random.normal(key, shape, jnp.float32)
    if pieces:
        values = values * level_of(key, shape, pieces, -0.22, 0.18)
    return jnp.clip(strengthened(values, jax.random.fold_in(key, 3), *heavy), -limit, limit).astype(kind)


def setup_inputs(seed: int = 0, part: int = 0) -> dict:
    key_of = jax.random.split(jax.random.key(seed), 8)
    part_splits = jax.random.split(jax.random.fold_in(key_of[7], part), 8)
    tokens = normal_values(part_splits[0], (TOKENS, MODEL_WIDTH), 1.0, 6.0, ((0, 4), (1, 4)))
    query_weight = heavy_noise(key_of[1], (MODEL_WIDTH, MODEL_WIDTH), MODEL_WIDTH ** -0.5, 0.125, ((1, 4),), (1, 0, 4, 2.0))
    adapter_down_maps = normal_values(key_of[2], (TENANT_COUNT, MODEL_WIDTH, ADAPTER_RANK), MODEL_WIDTH ** -0.5, 0.09375, ((0, 2), (1, 4)))
    adapter_up_maps = normal_values(key_of[3], (TENANT_COUNT, ADAPTER_RANK, MODEL_WIDTH), ADAPTER_RANK ** -0.5, 1.5, ((0, 2), (2, 4)))
    tenant_row_counts = draw_tenant_row_counts(jax.random.fold_in(jax.random.fold_in(key_of[7], part), 71), part)
    tenant_adapter_slot = jax.random.permutation(key_of[5], TENANT_COUNT).astype(jnp.int32)
    query_cotangent = normal_values(part_splits[6], (TOKENS, MODEL_WIDTH), 1.0, 6.0, ((0, 4), (1, 4)))
    return {"tokens": tokens, "query_weight": query_weight, "adapter_down_maps": adapter_down_maps, "adapter_up_maps": adapter_up_maps, "tenant_row_counts": tenant_row_counts, "tenant_adapter_slot": tenant_adapter_slot, "query_cotangent": query_cotangent}


adapter_scale = 2.0


def lookup(source, position):
    length = source.shape[0]
    match_mask = position[..., None] == jnp.arange(length, dtype=jnp.int32)
    return jnp.sum(jnp.where(match_mask, source, 0), axis=-1).astype(jnp.int32)


def layout(tenant_row_counts, row_ids):
    block_count = ((tenant_row_counts + BLOCK_ROWS - 1) // BLOCK_ROWS).astype(jnp.int32)
    segment_offset = (jnp.cumsum(block_count) - block_count).astype(jnp.int32)
    block_ids = row_ids // BLOCK_ROWS
    tenant_of = (jnp.sum((segment_offset[None, :] <= block_ids[:, None]).astype(jnp.int32), axis=1) - 1).astype(jnp.int32)
    offset = row_ids - BLOCK_ROWS * lookup(segment_offset, tenant_of)
    active_row_mask = offset < lookup(tenant_row_counts, tenant_of)
    return tenant_of, active_row_mask


def reference(tokens, query_weight, adapter_down_maps, adapter_up_maps, tenant_row_counts, tenant_adapter_slot, query_cotangent):
    highest_precision = lax.Precision.HIGHEST
    row_ids = jnp.arange(TOKENS, dtype=jnp.int32)
    tenant_of, active_row_mask = layout(tenant_row_counts, row_ids)
    tenant_hot = (tenant_of[:, None] == jnp.arange(TENANT_COUNT, dtype=jnp.int32)[None, :]).astype(jnp.float32)
    down_per_tenant = adapter_down_maps[tenant_adapter_slot].astype(jnp.float32)
    up_per_tenant = adapter_up_maps[tenant_adapter_slot].astype(jnp.float32)
    masked = jnp.where(active_row_mask[:, None], tokens, jnp.zeros_like(tokens))
    masked_function = masked.astype(jnp.float32)
    gradient_function = query_cotangent.astype(jnp.float32)
    base_query_output = jnp.dot(masked, query_weight, preferred_element_type=jnp.float32)
    low_all = jnp.einsum('rd,tdk->rtk', masked_function, down_per_tenant, precision=highest_precision)
    low_rank = jnp.einsum('rtk,rt->rk', low_all, tenant_hot, precision=highest_precision)
    low_b = low_rank.astype(jnp.bfloat16).astype(jnp.float32)
    back_all = jnp.einsum('rd,tkd->rtk', gradient_function, up_per_tenant, precision=highest_precision)
    derivative_inner_factor = jnp.einsum('rtk,rt->rk', back_all, tenant_hot, precision=highest_precision)
    back_b = derivative_inner_factor.astype(jnp.bfloat16).astype(jnp.float32)

    def add_tenant(totals, tenant_pos):
        result_grand_accumulation, input_gradient_total = totals
        select = tenant_hot[:, tenant_pos][:, None]
        result_grand_accumulation = result_grand_accumulation + select * jnp.dot(low_b, up_per_tenant[tenant_pos], precision=highest_precision)
        input_gradient_total = input_gradient_total + select * jnp.dot(back_b, down_per_tenant[tenant_pos].T, precision=highest_precision)
        return (result_grand_accumulation, input_gradient_total), None

    empty = jnp.zeros((TOKENS, MODEL_WIDTH), jnp.float32)
    (result_grand_accumulation, input_gradient_total), _ = lax.scan(add_tenant, (empty, empty), jnp.arange(TENANT_COUNT, dtype=jnp.int32))
    adapter_output = lax.optimization_barrier((adapter_scale * result_grand_accumulation).astype(jnp.bfloat16)).astype(jnp.float32)
    query = (base_query_output + adapter_output).astype(jnp.bfloat16)
    input_adapter_gradient = lax.optimization_barrier((adapter_scale * input_gradient_total).astype(jnp.bfloat16)).astype(jnp.float32)
    shard_width = MODEL_WIDTH // N_TENSOR

    def accumulate_piece(total, shard_pos):
        grad_cols = lax.dynamic_slice_in_dim(query_cotangent, shard_pos * shard_width, shard_width, 1)
        weight_cols = lax.dynamic_slice_in_dim(query_weight, shard_pos * shard_width, shard_width, 1)
        part_sum = lax.dot_general(grad_cols, weight_cols, (((1,), (1,)), ((), ())), preferred_element_type=jnp.float32)
        return total + lax.optimization_barrier(part_sum.astype(jnp.bfloat16)).astype(jnp.float32), None

    input_gradient_sum, _ = lax.scan(accumulate_piece, jnp.zeros((TOKENS, MODEL_WIDTH), jnp.float32), jnp.arange(N_TENSOR, dtype=jnp.int32))
    token_input_gradient = jnp.where(active_row_mask[:, None], input_gradient_sum + input_adapter_gradient, 0.0).astype(jnp.bfloat16)
    weight_grad = lax.dot_general(masked, query_cotangent, (((0,), (0,)), ((), ())), preferred_element_type=jnp.float32).astype(jnp.bfloat16)
    scaled_backward = tenant_hot[:, :, None] * back_b[:, None, :]
    tenant_down_map = adapter_scale * jnp.einsum('if,iqc->qfc', masked_function, scaled_backward, precision=highest_precision)
    scaled_low_rank = tenant_hot[:, :, None] * low_b[:, None, :]
    tenant_up_map = adapter_scale * jnp.einsum('mcw,mx->cwx', scaled_low_rank, gradient_function, precision=highest_precision)
    down_grad = jnp.zeros((TENANT_COUNT, MODEL_WIDTH, ADAPTER_RANK), jnp.float32).at[tenant_adapter_slot].set(tenant_down_map)
    up_grad = jnp.zeros((TENANT_COUNT, ADAPTER_RANK, MODEL_WIDTH), jnp.float32).at[tenant_adapter_slot].set(tenant_up_map)
    return (query, token_input_gradient, weight_grad, down_grad, up_grad)
```

```python
import jax
import jax.numpy as jnp
from jax import lax
from jax.sharding import PartitionSpec as P

BLOCK_ROWS = 128
SCALE = 2.0
F32 = jnp.float32
B16 = jnp.bfloat16


def dot(a, b, ca, cb):
    return lax.dot_general(a, b, (((ca,), (cb,)), ((), ())), preferred_element_type=F32)


def lookup(source, position):
    match_mask = position[..., None] == jnp.arange(source.shape[0], dtype=jnp.int32)
    return jnp.sum(jnp.where(match_mask, source, 0), axis=-1)


def layout(tenant_row_counts, row_ids):
    block_count = (tenant_row_counts + BLOCK_ROWS - 1) // BLOCK_ROWS
    segment_offset = jnp.cumsum(block_count) - block_count
    block_ids = row_ids // BLOCK_ROWS
    tenant_of = (
        jnp.sum((segment_offset[None, :] <= block_ids[:, None]).astype(jnp.int32), axis=1) - 1
    )
    offset = row_ids - BLOCK_ROWS * lookup(segment_offset, tenant_of)
    return tenant_of, offset < lookup(tenant_row_counts, tenant_of)


def rank_partials(maps, rows, mask, slots):
    every = dot(maps, rows, 1, 1)
    every = every.reshape(slots, -1, rows.shape[0])
    return jnp.sum(jnp.where(mask[:, None, :], every, 0.0), axis=0)


def spread(values, mask):
    wide = jnp.where(mask[:, None, :], values[None], jnp.zeros((), values.dtype))
    return wide.reshape(-1, values.shape[-1])


def shards_general(tokens, weight, down_maps, up_maps, counts, slot_of, cotangent):
    rows, width = tokens.shape
    held, _, rank = down_maps.shape
    slots = held * lax.axis_size("tenant")
    owner = lax.axis_index("tenant")
    row_ids = lax.axis_index(("tenant", "dp")) * rows + jnp.arange(rows, dtype=jnp.int32)
    tenant, live = layout(counts, row_ids)
    slot = lookup(slot_of, tenant)
    mask = slot[None, :] == jnp.arange(slots, dtype=jnp.int32)[:, None]
    grads = jnp.where(live[:, None], cotangent, jnp.zeros_like(cotangent))
    kept = jnp.where(live[:, None], tokens, jnp.zeros_like(tokens))
    down = lax.all_gather(jnp.swapaxes(down_maps, 1, 2), "tenant", axis=0, tiled=True)
    up = lax.all_gather(up_maps, "tenant", axis=0, tiled=True)
    down, up = down.reshape(-1, width), up.reshape(-1, width)
    gathered = lax.all_gather(kept, "tensor", axis=1, tiled=True)
    part = jnp.stack(
        [rank_partials(down, kept, mask, slots), rank_partials(up, grads, mask, slots)]
    )
    low, back = lax.psum(part.astype(B16), "tensor")
    low, back = spread(low, mask), spread(back, mask)
    base = dot(gathered, weight, 1, 0)
    query = (base + (SCALE * dot(low, up, 0, 0)).astype(B16).astype(F32)).astype(B16)
    term = dot(grads, weight, 1, 1).astype(B16)
    summed = lax.psum_scatter(term, "tensor", scatter_dimension=1, tiled=True).astype(F32)
    lora = (SCALE * dot(back, down, 0, 0)).astype(B16).astype(F32)
    token_grad = jnp.where(live[:, None], summed + lora, 0.0).astype(B16)
    axes = ("tenant", "dp")
    weight_grad = lax.psum(dot(gathered, grads, 0, 0).astype(B16), axes)
    maps = jnp.stack([SCALE * dot(back, kept, 1, 0), SCALE * dot(low, grads, 1, 0)])
    maps = lax.psum(maps.astype(B16), axes).astype(F32).reshape(2, slots, rank, width)
    maps = lax.dynamic_slice_in_dim(maps, owner * held, held, 1)
    return query, token_grad, weight_grad, jnp.swapaxes(maps[0], 1, 2), maps[1]


def arrival_plan(n):
    plan = [[] for _ in range(n - 1)]
    for z in range(n):
        seen = []
        for t in range(1, n):
            if z - t >= 0:
                seen.append((t, 0, z - t))
            if z + t < n:
                seen.append((t, 1, z + t))
        for step, entry in enumerate(seen):
            plan[step].append(entry)
    return plan


def shards_line(tokens, weight, down_maps, up_maps, counts, slot_of, cotangent):
    rows, width = tokens.shape
    held, _, rank = down_maps.shape
    n = lax.axis_size("tensor")
    slots = held * 2
    z = lax.axis_index("tensor")
    owner = lax.axis_index("tenant")
    core = lax.axis_index("dp")
    half = width // 2
    swap = [(0, 1), (1, 0)]

    def right(value, sources):
        return lax.ppermute(value, "tensor", [(i, i + 1) for i in sources])

    def left(value, sources):
        return lax.ppermute(value, "tensor", [(i, i - 1) for i in sources])

    def other_tenant(value):
        return lax.ppermute(value, "tenant", swap)

    def other_core(value):
        return lax.ppermute(value, "dp", swap)

    row_ids = (owner * 2 + core) * rows + jnp.arange(rows, dtype=jnp.int32)
    tenant, live = layout(counts, row_ids)
    place = lax.rem(lookup(slot_of, tenant) + (2 - owner) * held, slots)
    mask = place[None, :] == jnp.arange(slots, dtype=jnp.int32)[:, None]
    grads = jnp.where(live[:, None], cotangent, jnp.zeros_like(cotangent))

    first = (1 - core) * half
    second = core * half
    own = [
        lax.dynamic_slice_in_dim(tokens, first, half, 1),
        lax.dynamic_slice_in_dim(tokens, second, half, 1),
    ]

    from_left = {0: own}
    from_right = {0: own}
    for t in range(1, n):
        from_left[t] = [right(v, range(t - 1, n - 1)) for v in from_left[t - 1]]
        from_right[t] = [left(v, range(1, n - t + 1)) for v in from_right[t - 1]]

    mine = jnp.stack([jnp.swapaxes(down_maps, 1, 2), up_maps]).reshape(2, -1, width)
    fetched = other_tenant(lax.dynamic_index_in_dim(mine, core, 0, keepdims=False))
    shared = other_core(fetched)
    down = jnp.concatenate([mine[0], jnp.where(core == 0, fetched, shared)])
    up = jnp.concatenate([mine[1], jnp.where(core == 0, shared, fetched)])

    part = jnp.stack(
        [rank_partials(down, tokens, mask, slots), rank_partials(up, grads, mask, slots)]
    ).astype(B16)
    total = part.astype(F32)
    for k in range(1, n):
        total = total + lax.ppermute(
            part, "tensor", [(i, (i + k) % n) for i in range(n)]
        ).astype(F32)
    low, back = total.astype(B16)
    low, back = spread(low, mask), spread(back, mask)

    def weight_piece(pair):
        away = dot(pair[0], grads, 0, 0).astype(B16)
        home = dot(pair[1], grads, 0, 0)
        mix = (home + other_core(away).astype(F32)).astype(B16)
        subs = []
        for part_rows in jnp.split(mix, 2):
            whole = (part_rows.astype(F32) + other_tenant(part_rows).astype(F32)).astype(B16)
            subs.append((whole, other_core(whole)))
        return subs

    gathered = jnp.zeros((rows, n * width), B16)
    weight_grad = jnp.zeros((n * width, width), B16)

    def keep(gathered, weight_grad, pair, chunk):
        gathered = lax.dynamic_update_slice(gathered, pair[0], (0, chunk * width + first))
        gathered = lax.dynamic_update_slice(gathered, pair[1], (0, chunk * width + second))
        for i, (ours, theirs) in enumerate(weight_piece(pair)):
            at = chunk * width + i * (half // 2)
            weight_grad = lax.dynamic_update_slice(weight_grad, ours, (at + second, 0))
            weight_grad = lax.dynamic_update_slice(weight_grad, theirs, (at + first, 0))
        return gathered, weight_grad

    gathered, weight_grad = keep(gathered, weight_grad, own, z)
    for choices in arrival_plan(n):
        pair = None
        chunk = 0
        for at, (t, direction, source) in enumerate(choices):
            offer = (from_left, from_right)[direction][t]
            if pair is None:
                pair = offer
            else:
                pair = [jnp.where(z >= at, new, old) for new, old in zip(offer, pair)]
            chunk = jnp.where(z == at, source, chunk)
        gathered, weight_grad = keep(gathered, weight_grad, pair, chunk)

    base = dot(gathered, weight, 1, 0)
    lora_out = (SCALE * dot(low, up, 0, 0)).astype(B16).astype(F32)
    query = jnp.where(live[:, None], base + lora_out, 0.0).astype(B16)

    term = dot(grads, weight, 1, 1).astype(B16)
    pieces = jnp.split(term, 2)

    def term_of(piece, chunk):
        chunk = jnp.clip(chunk, 0, n - 1)
        return lax.dynamic_slice_in_dim(piece, chunk * width, width, 1)

    lora_in = (SCALE * dot(back, down, 0, 0)).astype(B16)
    results = []
    for piece, lora in zip(pieces, jnp.split(lora_in, 2)):
        sum_left = sum_right = None
        for t in range(2, n + 1):
            to_right = term_of(piece, n + z + 1 - t)
            to_left = term_of(piece, z - n - 1 + t)
            if sum_left is not None:
                to_right = (to_right.astype(F32) + sum_left.astype(F32)).astype(B16)
                to_left = (to_left.astype(F32) + sum_right.astype(F32)).astype(B16)
            sum_left = right(to_right, range(0, t - 1))
            sum_right = left(to_left, range(n + 1 - t, n))
        results.append(
            term_of(piece, z).astype(F32)
            + sum_left.astype(F32)
            + sum_right.astype(F32)
            + lora.astype(F32)
        )
    token_grad = jnp.where(live[:, None], jnp.concatenate(results), 0.0).astype(B16)

    maps = [SCALE * dot(back, tokens, 1, 0), SCALE * dot(low, grads, 1, 0)]
    for_sibling = jnp.where(core == 0, maps[1], maps[0]).astype(B16)
    summed = jnp.where(core == 0, maps[0], maps[1]) + other_core(for_sibling).astype(F32)
    kept, sent = jnp.split(summed, 2)
    kept = kept + other_tenant(sent.astype(B16)).astype(F32)
    sibling = other_core(kept)
    down_grad = jnp.where(core == 0, kept, sibling).reshape(held, rank, width)
    up_grad = jnp.where(core == 0, sibling, kept).reshape(held, rank, width)
    return query, token_grad, weight_grad, jnp.swapaxes(down_grad, 1, 2), up_grad


def solution(mesh):
    placed = (
        P(("groups", "tenant", "dp"), "tensor"),
        P(None, "tensor"),
        P("tenant", "tensor", None),
        P("tenant", None, "tensor"),
        P("groups"),
        P(),
        P(("groups", "tenant", "dp"), "tensor"),
    )
    short = 2 <= mesh.shape["tensor"] <= 4
    paired = mesh.shape["tenant"] == 2 and mesh.shape["dp"] == 2
    return jax.shard_map(
        shards_line if short and paired else shards_general,
        mesh=mesh,
        in_specs=placed,
        out_specs=(
            P(("groups", "tenant", "dp"), "tensor"),
            P(("groups", "tenant", "dp"), "tensor"),
            P("groups", "tensor"),
            P(("groups", "tenant"), "tensor", None),
            P(("groups", "tenant"), None, "tensor"),
        ),
        check_vma=False,
    )
```

```python
import functools

import jax
import jax.numpy as jnp
from jax import lax
from jax.experimental import pallas as pl
from jax.experimental.pallas import tpu as pltpu
from jax.sharding import PartitionSpec as P

BLOCK_ROWS = 128
SCALE = 2.0
F32 = jnp.float32
B16 = jnp.bfloat16


def dot(a, b, ca, cb):
    return lax.dot_general(a, b, (((ca,), (cb,)), ((), ())), preferred_element_type=F32)


def lookup(source, position):
    match_mask = position[..., None] == jnp.arange(source.shape[0], dtype=jnp.int32)
    return jnp.sum(jnp.where(match_mask, source, 0), axis=-1)


def layout(tenant_row_counts, row_ids):
    block_count = (tenant_row_counts + BLOCK_ROWS - 1) // BLOCK_ROWS
    segment_offset = jnp.cumsum(block_count) - block_count
    block_ids = row_ids // BLOCK_ROWS
    tenant_of = (
        jnp.sum((segment_offset[None, :] <= block_ids[:, None]).astype(jnp.int32), axis=1) - 1
    )
    offset = row_ids - BLOCK_ROWS * lookup(segment_offset, tenant_of)
    return tenant_of, offset < lookup(tenant_row_counts, tenant_of)


def rank_partials(maps, rows, mask, slots):
    every = dot(maps, rows, 1, 1)
    every = every.reshape(slots, -1, rows.shape[0])
    return jnp.sum(jnp.where(mask[:, None, :], every, 0.0), axis=0)


def spread(values, mask):
    wide = jnp.where(mask[:, None, :], values[None], jnp.zeros((), values.dtype))
    return wide.reshape(-1, values.shape[-1])


def shards_general(tokens, weight, down_maps, up_maps, counts, slot_of, cotangent):
    rows, width = tokens.shape
    held, _, rank = down_maps.shape
    slots = held * lax.axis_size("tenant")
    owner = lax.axis_index("tenant")
    row_ids = lax.axis_index(("tenant", "dp")) * rows + jnp.arange(rows, dtype=jnp.int32)
    tenant, live = layout(counts, row_ids)
    slot = lookup(slot_of, tenant)
    mask = slot[None, :] == jnp.arange(slots, dtype=jnp.int32)[:, None]
    grads = jnp.where(live[:, None], cotangent, jnp.zeros_like(cotangent))
    kept = jnp.where(live[:, None], tokens, jnp.zeros_like(tokens))
    down = lax.all_gather(jnp.swapaxes(down_maps, 1, 2), "tenant", axis=0, tiled=True)
    up = lax.all_gather(up_maps, "tenant", axis=0, tiled=True)
    down, up = down.reshape(-1, width), up.reshape(-1, width)
    gathered = lax.all_gather(kept, "tensor", axis=1, tiled=True)
    part = jnp.stack(
        [rank_partials(down, kept, mask, slots), rank_partials(up, grads, mask, slots)]
    )
    low, back = lax.psum(part.astype(B16), "tensor")
    low, back = spread(low, mask), spread(back, mask)
    base = dot(gathered, weight, 1, 0)
    query = (base + (SCALE * dot(low, up, 0, 0)).astype(B16).astype(F32)).astype(B16)
    term = dot(grads, weight, 1, 1).astype(B16)
    summed = lax.psum_scatter(term, "tensor", scatter_dimension=1, tiled=True).astype(F32)
    lora = (SCALE * dot(back, down, 0, 0)).astype(B16).astype(F32)
    token_grad = jnp.where(live[:, None], summed + lora, 0.0).astype(B16)
    axes = ("tenant", "dp")
    weight_grad = lax.psum(dot(gathered, grads, 0, 0).astype(B16), axes)
    maps = jnp.stack([SCALE * dot(back, kept, 1, 0), SCALE * dot(low, grads, 1, 0)])
    maps = lax.psum(maps.astype(B16), axes).astype(F32).reshape(2, slots, rank, width)
    maps = lax.dynamic_slice_in_dim(maps, owner * held, held, 1)
    return query, token_grad, weight_grad, jnp.swapaxes(maps[0], 1, 2), maps[1]


def arrival_plan(n):
    plan = [[] for _ in range(n - 1)]
    for z in range(n):
        seen = []
        for t in range(1, n):
            if z - t >= 0:
                seen.append((t, 0, z - t))
            if z + t < n:
                seen.append((t, 1, z + t))
        for step, entry in enumerate(seen):
            plan[step].append(entry)
    return plan


def whole(array):
    return pl.BlockSpec(array.shape, lambda *_: (0,) * array.ndim)


def call(body, table, grid, arrays, specs, outs, out_specs, scratch, flops, aliases=None):
    moved = sum(v.size * v.dtype.itemsize for v in arrays)
    return pl.pallas_call(
        body,
        grid_spec=pltpu.PrefetchScalarGridSpec(
            num_scalar_prefetch=1,
            grid=grid,
            in_specs=specs,
            out_specs=out_specs,
            scratch_shapes=scratch,
        ),
        out_shape=outs,
        input_output_aliases=aliases or {},
        compiler_params=pltpu.CompilerParams(vmem_limit_bytes=48 * 1024 * 1024),
        cost_estimate=pl.CostEstimate(flops=1, bytes_accessed=1, transcendentals=0),
    )(table, *arrays)


def hop_body(table, grads, weight, came, away, goes, share):
    share[...] = away[...]

    @pl.when(table[1] == 0)
    def _():
        goes[...] = came[...]

    @pl.when(table[1] != 0)
    def _():
        term = dot(grads[...], weight[...], 1, 1)
        goes[...] = (term + came[...].astype(F32)).astype(B16)


def hop(table, grads, weight, came):
    rows, width = came.shape
    half = width // 2
    cols = pl.BlockSpec((rows, half), lambda j, t: (0, j))
    return call(
        hop_body,
        table,
        (2,),
        [grads, weight, came, came],
        [
            whole(grads),
            pl.BlockSpec((half, width), lambda j, t: (2 * t[0] + j, 0)),
            cols,
            pl.BlockSpec((rows, half), lambda j, t: (0, t[2])),
        ],
        [jax.ShapeDtypeStruct((rows, width), B16), jax.ShapeDtypeStruct((rows, half), B16)],
        [cols, pl.BlockSpec((rows, half), lambda j, t: (0, 0))],
        [],
        0,
    )


def copy_chosen(choice, offers, target):
    if len(offers) == 1:
        target[...] = offers[0][...]
        return
    for at, offer in enumerate(offers):

        @pl.when(choice == at)
        def _(offer=offer):
            target[...] = offer[...]


def half_spec(array, half, core_at):
    if array.shape[1] == half:
        return whole(array)
    return pl.BlockSpec((array.shape[0], half), lambda j, t: (0, t[core_at]))


def piece_body(count, table, *refs):
    ours, theirs = refs[:count], refs[count : 2 * count]
    grads, their_grads, out, a, b = refs[2 * count :]

    @pl.when(pl.program_id(0) == 0)
    def _():
        copy_chosen(table[0], ours, a)
        copy_chosen(table[0], theirs, b)

    out[...] = (
        dot(a[...], grads[...], 0, 0) + dot(b[...], their_grads[...], 0, 0)
    ).astype(B16)


def piece(table, ours, theirs, grads, their_grads):
    rows, width = grads.shape
    half = width // 2
    cols = pl.BlockSpec((rows, width // 2), lambda j, t: (0, j))
    return call(
        functools.partial(piece_body, len(ours)),
        table,
        (2,),
        [*ours, *theirs, grads, their_grads],
        [half_spec(v, half, 1) for v in (*ours, *theirs)] + [cols, cols],
        jax.ShapeDtypeStruct((half, width), B16),
        pl.BlockSpec((half, width // 2), lambda j, t: (0, j)),
        [pltpu.VMEM((rows, half), B16)] * 2,
        0,
    )


def query_body(groups, n, half, table, *refs):
    offers, blocks = refs[: -5 - n], refs[-5 - n : -5]
    own_out, other_out, rows_in, weight_in, _ = refs[-5:]
    rows = own_out.shape[0]

    @pl.when(pl.program_id(0) == 0)
    def _():
        at = 0
        for step, count in enumerate(groups):
            start = pl.multiple_of(table[1 + step] * half, half)
            for side in range(2):
                here = offers[at : at + count]
                at += count
                target = rows_in.at[pl.ds(side * rows, rows), pl.ds(start, half)]
                copy_chosen(table[1 + n + step], here, target)

    for chunk in range(n):
        weight_in[pl.ds(chunk * half, half), :] = blocks[chunk][...]
    own_out[...] = dot(rows_in[pl.ds(0, rows), :], weight_in[...], 1, 0)
    other_out[...] = dot(rows_in[pl.ds(rows, rows), :], weight_in[...], 1, 0).astype(B16)


def query_parts(table, offers, weight):
    n = len(offers)
    rows, width = offers[0][0][0].shape[0], weight.shape[1]
    half = cols = width // 2
    flat = [v for pair in offers for side in pair for v in side]

    def block(chunk):
        return pl.BlockSpec((half, cols), lambda j, t: (2 * chunk + t[0], j))

    out = pl.BlockSpec((rows, cols), lambda j, t: (0, j))
    return call(
        functools.partial(query_body, [len(pair[0]) for pair in offers], n, half),
        table,
        (2,),
        [*flat] + [weight] * n,
        [half_spec(v, half, 0) for v in flat] + [block(c) for c in range(n)],
        [
            jax.ShapeDtypeStruct((rows, width), F32),
            jax.ShapeDtypeStruct((rows, width), B16),
        ],
        [out, out],
        [
            pltpu.VMEM((2 * rows, n * half), B16),
            pltpu.VMEM((n * half, cols), B16),
            pltpu.VMEM((8, 128), F32),
        ],
        0,
    )


def term_body(table, grads, weight, out):
    out[...] = dot(grads[...], weight[...], 1, 1).astype(B16)


def term_of(table, grads, weight):
    rows, width = grads.shape
    half = width // 2
    return call(
        term_body,
        table,
        (2,),
        [grads, weight],
        [whole(grads), pl.BlockSpec((half, width), lambda j, t: (2 * t[0] + j, 0))],
        jax.ShapeDtypeStruct((rows, width), B16),
        pl.BlockSpec((rows, half), lambda j, t: (0, j)),
        [],
        2 * rows * width * width,
    )


def place_body(table, ours, theirs, *refs):
    out = refs[-1]

    @pl.when(pl.program_id(0) == 0)
    def _():
        out[...] = ours[...]

    @pl.when(pl.program_id(0) == 1)
    def _():
        out[...] = theirs[...]


def place(table, ours, theirs, target, shape):
    half, width = ours.shape
    arrays, specs, aliases = [ours, theirs], [whole(ours), whole(theirs)], {}
    if target is not None:
        arrays.append(target)
        specs.append(pl.BlockSpec(memory_space=pl.ANY))
        aliases = {3: 0}
    return call(
        place_body,
        table,
        (2,),
        arrays,
        specs,
        jax.ShapeDtypeStruct(shape, B16),
        pl.BlockSpec((half, width), lambda i, t: (t[i], 0)),
        [],
        0,
        aliases,
    )


def add_body(table, a, b, out):
    out[...] = (a[...].astype(F32) + b[...].astype(F32)).astype(B16)


def add(a, b):
    rows, width = a.shape
    steps = 2 if rows >= 256 else 1
    spec = pl.BlockSpec((rows // steps, width), lambda i, t: (i, 0))
    out = jax.ShapeDtypeStruct(a.shape, B16)
    return call(add_body, jnp.zeros((1,), jnp.int32), (steps,), [a, b], [spec] * 2, out, spec, [], 0)


def ranks_body(rank, table, mine, fetched, shared, relative, tokens, grads, down, up, part):
    split = mine.shape[1]
    down[pl.ds(0, split), :] = mine[0]
    up[pl.ds(0, split), :] = mine[1]

    @pl.when(table[0] == 0)
    def _():
        down[pl.ds(split, split), :] = fetched[...]
        up[pl.ds(split, split), :] = shared[...]

    @pl.when(table[0] != 0)
    def _():
        down[pl.ds(split, split), :] = shared[...]
        up[pl.ds(split, split), :] = fetched[...]

    for kind, (maps, rows) in enumerate(((down, tokens), (up, grads))):
        every = dot(maps[...], rows[...], 1, 1)
        total = None
        for slot in range(2 * split // rank):
            own = jnp.where(relative[...] == slot, every[slot * rank : (slot + 1) * rank], 0.0)
            total = own if total is None else total + own
        part[pl.ds(kind * rank, rank), :] = total.astype(B16)


def ranks_of(table, rank, mine, fetched, shared, relative, tokens, grads):
    rows, width = tokens.shape
    arrays = [mine, fetched, shared, relative, tokens, grads]
    outs = [
        jax.ShapeDtypeStruct((2 * mine.shape[1], width), B16),
        jax.ShapeDtypeStruct((2 * mine.shape[1], width), B16),
        jax.ShapeDtypeStruct((2 * rank, rows), B16),
    ]
    body = functools.partial(ranks_body, rank)
    specs = [whole(v) for v in arrays]
    return call(body, table, (1,), arrays, specs, outs, [whole(v) for v in outs], [], 0)


def maps_body(rank, table, part, came, relative, tokens, grads, low, back, kept, sent):
    total = (part[...].astype(F32) + came[...].astype(F32)).astype(B16).astype(F32)
    for kind, wide in enumerate((low, back)):
        own = total[kind * rank : (kind + 1) * rank]
        for slot in range(wide.shape[0] // rank):
            spread_out = jnp.where(relative[...] == slot, own, 0.0)
            wide[pl.ds(slot * rank, rank), :] = spread_out.astype(B16)
    for kind, (wide, rows) in enumerate(((back, tokens), (low, grads))):
        term = SCALE * dot(wide[...], rows[...], 1, 0)

        @pl.when(table[0] == kind)
        def _(term=term):
            kept[...] = term

        @pl.when(table[0] != kind)
        def _(term=term):
            sent[...] = term.astype(B16)


def maps_of(table, rank, slots, part, came, relative, tokens, grads):
    rows, width = tokens.shape
    arrays = [part, came, relative, tokens, grads]
    outs = [
        jax.ShapeDtypeStruct((slots * rank, rows), B16),
        jax.ShapeDtypeStruct((slots * rank, rows), B16),
        jax.ShapeDtypeStruct((slots * rank, width), F32),
        jax.ShapeDtypeStruct((slots * rank, width), B16),
    ]
    body = functools.partial(maps_body, rank)
    specs = [whole(v) for v in arrays]
    return call(body, table, (1,), arrays, specs, outs, [whole(v) for v in outs], [], 0)


def lora_body(table, low, up, back, down, out, into):
    out[...] = (SCALE * dot(low[...], up[...], 0, 0)).astype(B16)
    into[...] = (SCALE * dot(back[...], down[...], 0, 0)).astype(B16)


def lora_of(low, up, back, down):
    rows, width = low.shape[1], up.shape[1]
    arrays = [low, up, back, down]
    out = jax.ShapeDtypeStruct((rows, width), B16)
    specs = [whole(v) for v in arrays]
    table = jnp.zeros((1,), jnp.int32)
    return call(lora_body, table, (1,), arrays, specs, [out, out], [whole(out)] * 2, [], 0)


def finish_body(table, here, there, lora, live, out):
    total = here[...] + there[...].astype(F32) + lora[...].astype(F32)
    out[...] = jnp.where(live[...] > 0, total, 0.0).astype(B16)


def finish(here, there, lora, live):
    rows, width = here.shape
    spec = pl.BlockSpec((rows // 2, width), lambda i, t: (i, 0))
    thin = pl.BlockSpec((rows // 2, 1), lambda i, t: (i, 0))
    out = jax.ShapeDtypeStruct((rows, width), B16)
    arrays = [here, there, lora, live]
    table = jnp.zeros((1,), jnp.int32)
    return call(finish_body, table, (2,), arrays, [spec] * 3 + [thin], out, spec, [], 0)


def shards_line(tokens, weight, down_maps, up_maps, counts, slot_of, cotangent):
    rows, width = tokens.shape
    held, _, rank = down_maps.shape
    n = lax.axis_size("tensor")
    slots = held * 2
    z = lax.axis_index("tensor")
    owner = lax.axis_index("tenant")
    core = lax.axis_index("dp")
    swap = [(0, 1), (1, 0)]
    ahead = jnp.where(core == 0, z, n - 1 - z)
    line_pairs = []
    for i in range(n - 1):
        line_pairs += [(2 * i, 2 * i + 2), (2 * i + 3, 2 * i + 1)]

    def along(value):
        return lax.ppermute(value, ("tensor", "dp"), line_pairs)

    def other_tenant(value):
        return lax.ppermute(value, "tenant", swap)

    def other_core(value):
        return lax.ppermute(value, "dp", swap)

    def other_core_halves(value):
        return jnp.concatenate([other_core(v) for v in jnp.split(value, 2)])

    def numbers(*values):
        return jnp.stack([v.astype(jnp.int32) for v in values])

    chunk_of = [z]
    choice_of = [jnp.zeros((), jnp.int32)]
    kinds_of = [None]
    for choices in arrival_plan(n):
        kinds = sorted({(t, d == c) for t, d, _ in choices for c in range(2)})
        chunk = choice = jnp.zeros((), jnp.int32)
        for at, (t, direction, source) in enumerate(choices):
            chunk = jnp.where(z == at, source, chunk)
            for c in range(2):
                here = (z == at) & (core == c)
                choice = jnp.where(here, kinds.index((t, direction == c)), choice)
        chunk_of.append(chunk)
        choice_of.append(choice)
        kinds_of.append(kinds)

    st = {}

    def fence():
        names = list(st)
        st.update(zip(names, lax.optimization_barrier([st[name] for name in names])))

    def hop_of(k):
        t, side = k // 2 + 1, k % 2
        chunk = jnp.clip(n + ahead + 1 - t, 0, n - 1)
        chunk = jnp.where(core == 0, chunk, n - 1 - chunk)
        sums = (ahead < n - 1) & (ahead < t - 1)
        table = numbers(chunk, sums, 1 - core)
        grads = st["their_grads" if side else "grads"]
        st["sent"], st["share"] = hop(table, grads, st["weight"], st["line", t - 1, side])

    def offers_of(step):
        if step == 0:
            return [[st["tokens"]], [st["their_tokens"]]]
        kinds = kinds_of[step]
        return [
            [st["line", t, s] if mine else st["shared", t, 1 - s] for t, mine in kinds]
            for s in range(2)
        ]

    def piece_of(step):
        table = numbers(choice_of[step], core)
        st["mix", step] = piece(table, *offers_of(step), st["grads"], st["their_grads"])

    def sum_of(step):
        st["ours", step] = add(st.pop(("mix", step)), st.pop(("x", step)))

    def place_of(step, theirs):
        blocks = numbers(2 * chunk_of[step] + core, 2 * chunk_of[step] + 1 - core)
        into = st.get("wg")
        st["wg"] = place(blocks, st.pop(("ours", step)), theirs, into, (n * width, width))

    st["weight"], st["tokens"] = weight, tokens
    line = along(tokens)
    st["their_tokens"] = other_core(tokens)
    theirs = other_core(cotangent)
    mine = jnp.stack([jnp.swapaxes(down_maps, 1, 2), up_maps]).reshape(2, -1, width)
    st["fetched"] = other_tenant(lax.dynamic_index_in_dim(mine, core, 0, keepdims=False))
    st["mine"] = mine
    row_ids = (owner * 2 + core) * rows + jnp.arange(rows, dtype=jnp.int32)
    tenant, live = layout(counts, row_ids)
    relative = lax.rem(lookup(slot_of, tenant) + (2 - owner) * held, slots)
    st["relative"] = relative[None, :]
    st["live"] = live.astype(F32)[:, None]
    their_live = layout(counts, row_ids + (1 - 2 * core) * rows)[1]
    st["grads"] = jnp.where(live[:, None], cotangent, jnp.zeros_like(cotangent))
    st["their_grads"] = jnp.where(their_live[:, None], theirs, jnp.zeros_like(cotangent))
    fence()

    coming = along(st["their_tokens"])
    piece_of(0)
    swapped = other_tenant(st["mix", 0])
    shared = other_core(st["fetched"])
    st["term"] = term_of(z[None], st["grads"], st["weight"])
    names = ("relative", "tokens", "grads")
    st["down"], st["up"], st["part"] = ranks_of(
        core[None], rank, st.pop("mine"), st.pop("fetched"), shared, *[st[v] for v in names]
    )
    st["line", 1, 0] = line
    line = coming
    fence()

    wg_share = None
    for k in range(2, 2 * n + 1):
        t, side, step = k // 2 + 1, k % 2, k // 2
        last = k == 2 * n
        if not last:
            hop_of(k)
        if side == 1:
            st["x", step - 1] = swapped
        if k in (2, 3):
            pairs = [(i, i ^ (k - 1)) for i in range(n)]
            st["came"] = lax.ppermute(st["part"], "tensor", pairs)
        if k == 4:
            st["maps"] = st["maps"] + other_core(st.pop("for_sibling")).astype(F32)
        if k == 6:
            kept, sent = jnp.split(st.pop("maps"), 2)
            st["kept"] = kept + other_tenant(sent.astype(B16)).astype(F32)
        if last:
            kept = st.pop("kept")
            other = other_core(kept)
            down_grad = jnp.where(core == 0, kept, other).reshape(held, rank, width)
            st["up_grad"] = jnp.where(core == 0, other, kept).reshape(held, rank, width)
            st["down_grad"] = jnp.swapaxes(down_grad, 1, 2)
        fence()
        if not last:
            coming = along(st.pop("sent"))
            st["shared", t - 1, side] = other_core(st.pop("share"))
        if side == 1:
            piece_of(step)
            swapped = other_tenant(st["mix", step])
            sum_of(step - 1)
        elif 4 <= k < 2 * n:
            wg_share = other_core(st["ours", step - 2])
        if k >= 6 and side == 0:
            place_of(step - 3, st.pop("theirs"))
        if k == 2:
            st["part"] = add(st["part"], st.pop("came"))
        if k == 3:
            st["low"], st["back"], st["maps"], st["for_sibling"] = maps_of(
                core[None],
                rank,
                slots,
                st.pop("part"),
                st.pop("came"),
                *[st[v] for v in names],
            )
        if k == 4:
            maps = [st.pop(v) for v in ("low", "up", "back", "down")]
            st["lora_out"], st["lora_in"] = lora_of(*maps)
        if last:
            offers = [offers_of(s) for s in range(n)]
            table = numbers(core, *chunk_of, *choice_of)
            st["query_here"], st["query_there"] = query_parts(table, offers, st["weight"])
        st["line", (k - 1) // 2 + 1, 1 - side] = line
        line = coming
        if side == 1 and wg_share is not None:
            st["theirs"] = wg_share
            wg_share = None
        fence()

    theirs = other_core_halves(st["line", n, 1])
    there = other_core_halves(st.pop("query_there"))
    total = st.pop("term").astype(F32) + st.pop("lora_in").astype(F32)
    total = total + st["line", n, 0].astype(F32) + theirs.astype(F32)
    st["token_grad"] = total.astype(B16)
    st["query"] = finish(st.pop("query_here"), there, st.pop("lora_out"), st.pop("live"))
    fence()
    st["x", n - 1] = swapped
    fence()
    sum_of(n - 1)
    shares = [other_core(st["ours", step]) for step in (n - 2, n - 1)]
    for step in (n - 2, n - 1):
        place_of(step, shares[step - n + 2])
    return st["query"], st["token_grad"], st["wg"], st["down_grad"], st["up_grad"]


def solution(mesh):
    placed = (
        P(("groups", "tenant", "dp"), "tensor"),
        P(None, "tensor"),
        P("tenant", "tensor", None),
        P("tenant", None, "tensor"),
        P("groups"),
        P(),
        P(("groups", "tenant", "dp"), "tensor"),
    )
    short = mesh.shape["tensor"] == 4
    paired = mesh.shape["tenant"] == 2 and mesh.shape["dp"] == 2
    return jax.shard_map(
        shards_line if short and paired else shards_general,
        mesh=mesh,
        in_specs=placed,
        out_specs=(
            P(("groups", "tenant", "dp"), "tensor"),
            P(("groups", "tenant", "dp"), "tensor"),
            P("groups", "tensor"),
            P(("groups", "tenant"), "tensor", None),
            P(("groups", "tenant"), None, "tensor"),
        ),
        check_vma=False,
    )
```

```python
import functools

import jax
import jax.numpy as jnp
from jax import lax
from jax.experimental import pallas as pl
from jax.experimental.pallas import tpu as pltpu
from jax.sharding import PartitionSpec as P

BLOCK_ROWS = 128
SCALE = 2.0
F32 = jnp.float32
B16 = jnp.bfloat16


def dot(a, b, ca, cb):
    return lax.dot_general(a, b, (((ca,), (cb,)), ((), ())), preferred_element_type=F32)


def lookup(source, position):
    match_mask = position[..., None] == jnp.arange(source.shape[0], dtype=jnp.int32)
    return jnp.sum(jnp.where(match_mask, source, 0), axis=-1)


def layout(tenant_row_counts, row_ids):
    block_count = (tenant_row_counts + BLOCK_ROWS - 1) // BLOCK_ROWS
    segment_offset = jnp.cumsum(block_count) - block_count
    block_ids = row_ids // BLOCK_ROWS
    tenant_of = (
        jnp.sum((segment_offset[None, :] <= block_ids[:, None]).astype(jnp.int32), axis=1) - 1
    )
    offset = row_ids - BLOCK_ROWS * lookup(segment_offset, tenant_of)
    return tenant_of, offset < lookup(tenant_row_counts, tenant_of)


def rank_partials(maps, rows, mask, slots):
    every = dot(maps, rows, 1, 1)
    every = every.reshape(slots, -1, rows.shape[0])
    return jnp.sum(jnp.where(mask[:, None, :], every, 0.0), axis=0)


def spread(values, mask):
    wide = jnp.where(mask[:, None, :], values[None], jnp.zeros((), values.dtype))
    return wide.reshape(-1, values.shape[-1])


def shards_general(tokens, weight, down_maps, up_maps, counts, slot_of, cotangent):
    rows, width = tokens.shape
    held, _, rank = down_maps.shape
    slots = held * lax.axis_size("tenant")
    owner = lax.axis_index("tenant")
    row_ids = lax.axis_index(("tenant", "dp")) * rows + jnp.arange(rows, dtype=jnp.int32)
    tenant, live = layout(counts, row_ids)
    slot = lookup(slot_of, tenant)
    mask = slot[None, :] == jnp.arange(slots, dtype=jnp.int32)[:, None]
    grads = jnp.where(live[:, None], cotangent, jnp.zeros_like(cotangent))
    kept = jnp.where(live[:, None], tokens, jnp.zeros_like(tokens))
    down = lax.all_gather(jnp.swapaxes(down_maps, 1, 2), "tenant", axis=0, tiled=True)
    up = lax.all_gather(up_maps, "tenant", axis=0, tiled=True)
    down, up = down.reshape(-1, width), up.reshape(-1, width)
    gathered = lax.all_gather(kept, "tensor", axis=1, tiled=True)
    part = jnp.stack(
        [rank_partials(down, kept, mask, slots), rank_partials(up, grads, mask, slots)]
    )
    low, back = lax.psum(part.astype(B16), "tensor")
    low, back = spread(low, mask), spread(back, mask)
    base = dot(gathered, weight, 1, 0)
    query = (base + (SCALE * dot(low, up, 0, 0)).astype(B16).astype(F32)).astype(B16)
    term = dot(grads, weight, 1, 1).astype(B16)
    summed = lax.psum_scatter(term, "tensor", scatter_dimension=1, tiled=True).astype(F32)
    lora = (SCALE * dot(back, down, 0, 0)).astype(B16).astype(F32)
    token_grad = jnp.where(live[:, None], summed + lora, 0.0).astype(B16)
    axes = ("tenant", "dp")
    weight_grad = lax.psum(dot(gathered, grads, 0, 0).astype(B16), axes)
    maps = jnp.stack([SCALE * dot(back, kept, 1, 0), SCALE * dot(low, grads, 1, 0)])
    maps = lax.psum(maps.astype(B16), axes).astype(F32).reshape(2, slots, rank, width)
    maps = lax.dynamic_slice_in_dim(maps, owner * held, held, 1)
    return query, token_grad, weight_grad, jnp.swapaxes(maps[0], 1, 2), maps[1]


def arrival_plan(n):
    plan = [[] for _ in range(n - 1)]
    for z in range(n):
        seen = []
        for t in range(1, n):
            if z - t >= 0:
                seen.append((t, 0, z - t))
            if z + t < n:
                seen.append((t, 1, z + t))
        for step, entry in enumerate(seen):
            plan[step].append(entry)
    return plan


def whole(array):
    return pl.BlockSpec(array.shape, lambda *_: (0,) * array.ndim)


def call(body, table, grid, arrays, specs, outs, out_specs, scratch, flops, aliases=None, limit=48):
    moved = sum(v.size * v.dtype.itemsize for v in arrays)
    return pl.pallas_call(
        body,
        grid_spec=pltpu.PrefetchScalarGridSpec(
            num_scalar_prefetch=1,
            grid=grid,
            in_specs=specs,
            out_specs=out_specs,
            scratch_shapes=scratch,
        ),
        out_shape=outs,
        input_output_aliases=aliases or {},
        compiler_params=pltpu.CompilerParams(vmem_limit_bytes=limit * 1024 * 1024),
        cost_estimate=pl.CostEstimate(flops=1, bytes_accessed=1, transcendentals=0),
    )(table, *arrays)


FREE = ()
HOP_STEPS = 2


def hop_body(table, grads, weight, came, goes, share):
    @pl.when(pl.program_id(0) == table[2])
    def _():
        share[...] = came[...]

    @pl.when(table[1] == 0)
    def _():
        goes[...] = came[...]

    @pl.when(table[1] != 0)
    def _():
        term = dot(grads[...], weight[...], 1, 1)
        goes[...] = (term + came[...].astype(F32)).astype(B16)


def hop(table, grads, weight, came):
    rows, width = came.shape
    half, step = width // 2, width // HOP_STEPS
    cols = pl.BlockSpec((rows, step), lambda j, t: (0, j))
    return call(
        hop_body,
        table,
        (HOP_STEPS,),
        [grads, weight, came],
        [
            whole(grads),
            pl.BlockSpec((step, width), lambda j, t: (HOP_STEPS * t[0] + j, 0)),
            cols,
        ],
        [jax.ShapeDtypeStruct((rows, width), B16), jax.ShapeDtypeStruct((rows, half), B16)],
        [cols, pl.BlockSpec((rows, half), lambda j, t: (0, 0))],
        [],
        0,
    )


def start_chosen(choice, offers, core, target, done):
    rows, half = target.shape
    for at, offer in enumerate(offers):

        @pl.when(choice == at)
        def _(offer=offer):
            source = offer
            if offer.shape[1] != half:
                source = offer.at[:, pl.ds(pl.multiple_of(core * half, half), half)]
            pltpu.make_async_copy(source, target, done).start()


def wait_chosen(target, done):
    pltpu.make_async_copy(target, target, done).wait()


def piece_body(count, extra, table, *refs):
    ours, theirs = refs[:count], refs[count : 2 * count]
    grads, their_grads = refs[2 * count : 2 * count + 2]
    rest = refs[2 * count + 2 :]
    out, a, b, done = rest[2 * extra], *rest[-3:]
    half = a.shape[1]

    @pl.when(pl.program_id(0) == 0)
    def _():
        start_chosen(table[0], ours, table[1], a, done.at[0])
        start_chosen(table[0], theirs, table[1], b, done.at[1])
        wait_chosen(a, done.at[0])
        wait_chosen(b, done.at[1])

    mix = dot(a[...], grads[...], 0, 0) + dot(b[...], their_grads[...], 0, 0)
    out[...] = mix.astype(B16)
    if extra:
        maps, came, kept, sent = rest[0], rest[1], rest[3], rest[4]
        split = kept.shape[0]
        total = maps[...] + came[...].astype(F32)
        kept[...] = total[:split]
        sent[...] = total[split:].astype(B16)


def piece(table, ours, theirs, grads, their_grads, extra=()):
    rows, width = grads.shape
    half = width // 2

    def cols(count):
        return pl.BlockSpec((count, width // 2), lambda j, t: (0, j))

    split = extra[0].shape[0] // 2 if extra else 0
    outs = [jax.ShapeDtypeStruct((half, width), B16)]
    if extra:
        outs.append(jax.ShapeDtypeStruct((split, width), F32))
        outs.append(jax.ShapeDtypeStruct((split, width), B16))
    return call(
        functools.partial(piece_body, len(ours), 1 if extra else 0),
        table,
        (2,),
        [*ours, *theirs, grads, their_grads, *extra],
        [pl.BlockSpec(memory_space=pltpu.HBM)] * (2 * len(ours))
        + [cols(rows), cols(rows)]
        + [cols(2 * split)] * len(extra),
        outs,
        [cols(v.shape[0]) for v in outs],
        [pltpu.VMEM((rows, half), B16)] * 2 + [pltpu.SemaphoreType.DMA((2,))],
        0,
    )


def query_body(groups, n, half, table, *refs):
    offers, blocks = refs[: -6 - n], refs[-6 - n : -6]
    own_out, other_out, other_end, rows_in, weight_in, done = refs[-6:]
    rows = own_out.shape[0]

    @pl.when(pl.program_id(0) == 0)
    def _():
        at = 0
        waits = []
        for step, count in enumerate(groups):
            start = pl.multiple_of(table[1 + step] * half, half)
            for side in range(2):
                here = offers[at : at + count]
                at += count
                target = rows_in.at[pl.ds(side * rows, rows), pl.ds(start, half)]
                sem = done.at[2 * step + side]
                start_chosen(table[1 + n + step], here, table[0], target, sem)
                waits.append((target, sem))
        for target, sem in waits:
            wait_chosen(target, sem)

    for chunk in range(n):
        weight_in[pl.ds(chunk * half, half), :] = blocks[chunk][...]
    own_out[...] = dot(rows_in[pl.ds(0, rows), :], weight_in[...], 1, 0)
    other = dot(rows_in[pl.ds(rows, rows), :], weight_in[...], 1, 0).astype(B16)
    other_out[...] = other[: rows // 2]
    other_end[...] = other[rows // 2 :]


def query_parts(table, offers, weight):
    n = len(offers)
    rows, width = offers[0][0][0].shape[0], weight.shape[1]
    half = cols = width // 2
    flat = [v for pair in offers for side in pair for v in side]

    def block(chunk):
        return pl.BlockSpec((half, cols), lambda j, t: (2 * chunk + t[0], j))

    out = pl.BlockSpec((rows, cols), lambda j, t: (0, j))
    part = pl.BlockSpec((rows // 2, cols), lambda j, t: (0, j))
    return call(
        functools.partial(query_body, [len(pair[0]) for pair in offers], n, half),
        table,
        (2,),
        [*flat] + [weight] * n,
        [pl.BlockSpec(memory_space=pltpu.HBM)] * len(flat) + [block(c) for c in range(n)],
        [
            jax.ShapeDtypeStruct((rows, width), F32),
            jax.ShapeDtypeStruct((rows // 2, width), B16),
            jax.ShapeDtypeStruct((rows // 2, width), B16),
        ],
        [out, part, part],
        [
            pltpu.VMEM((2 * rows, n * half), B16),
            pltpu.VMEM((n * half, cols), B16),
            pltpu.SemaphoreType.DMA((2 * n,)),
        ],
        0,
        limit=28,
    )


def term_body(table, grads, weight, out):
    out[...] = dot(grads[...], weight[...], 1, 1).astype(B16)


def term_of(table, grads, weight):
    rows, width = grads.shape
    half = width // 2
    return call(
        term_body,
        table,
        (2,),
        [grads, weight],
        [whole(grads), pl.BlockSpec((half, width), lambda j, t: (2 * t[0] + j, 0))],
        jax.ShapeDtypeStruct((rows, width), B16),
        pl.BlockSpec((rows, half), lambda j, t: (0, j)),
        [],
        2 * rows * width * width,
    )


def into_target(value, target, shape, at, body, extra, outs, steps):
    rows, width = shape[2], shape[1]
    block = rows // steps
    spec = pl.BlockSpec((block, width), lambda i, t: (i, 0))
    arrays, specs, aliases = [value, *extra], [spec] * (1 + len(extra)), {}
    if target is not None:
        aliases = {1 + len(arrays): 0}
        arrays.append(target)
        specs.append(pl.BlockSpec(memory_space=pl.ANY))
    where = pl.BlockSpec((block, width), lambda i, t: (steps * t[0] + i, 0))
    return call(
        body,
        at,
        (steps,),
        arrays,
        specs,
        [jax.ShapeDtypeStruct(shape[:2], B16)] + [jax.ShapeDtypeStruct((rows, width), B16)] * outs,
        [where] + [spec] * outs,
        [],
        0,
        aliases,
    )


def place_body(table, value, *refs):
    refs[-1][...] = value[...]


def place(at, value, target, shape):
    return into_target(value, target, (*shape, value.shape[0]), at, place_body, (), 0, 2)[0]


def sum_body(table, a, b, *refs):
    total = (a[...].astype(F32) + b[...].astype(F32)).astype(B16)
    refs[-2][...] = total
    refs[-1][...] = total


def place_sum(at, a, b, target, shape, rows):
    return into_target(a, target, (*shape, rows), at, sum_body, (b,), 1, 2)


def ranks_body(rank, table, mine, fetched, shared, relative, tokens, grads, down, up, part):
    split = mine.shape[1]
    down[pl.ds(0, split), :] = mine[0]
    up[pl.ds(0, split), :] = mine[1]

    @pl.when(table[0] == 0)
    def _():
        down[pl.ds(split, split), :] = fetched[...]
        up[pl.ds(split, split), :] = shared[...]

    @pl.when(table[0] != 0)
    def _():
        down[pl.ds(split, split), :] = shared[...]
        up[pl.ds(split, split), :] = fetched[...]

    for kind, (maps, rows) in enumerate(((down, tokens), (up, grads))):
        every = dot(maps[...], rows[...], 1, 1)
        total = None
        for slot in range(2 * split // rank):
            own = jnp.where(relative[...] == slot, every[slot * rank : (slot + 1) * rank], 0.0)
            total = own if total is None else total + own
        part[pl.ds(kind * rank, rank), :] = total.astype(B16)


def ranks_of(table, rank, mine, fetched, shared, relative, tokens, grads):
    rows, width = tokens.shape
    arrays = [mine, fetched, shared, relative, tokens, grads]
    outs = [
        jax.ShapeDtypeStruct((2 * mine.shape[1], width), B16),
        jax.ShapeDtypeStruct((2 * mine.shape[1], width), B16),
        jax.ShapeDtypeStruct((2 * rank, rows), B16),
    ]
    body = functools.partial(ranks_body, rank)
    specs = [whole(v) for v in arrays]
    return call(body, table, (1,), arrays, specs, outs, [whole(v) for v in outs], [], 0)


def maps_body(rank, count, table, *refs):
    relative, tokens, grads, low, back, kept, sent = refs[count:]
    total = refs[0][...].astype(F32)
    for part in refs[1:count]:
        total += part[...].astype(F32)
    total = total.astype(B16).astype(F32)
    for kind, wide in enumerate((low, back)):
        own = total[kind * rank : (kind + 1) * rank]
        for slot in range(wide.shape[0] // rank):
            spread_out = jnp.where(relative[...] == slot, own, 0.0)
            wide[pl.ds(slot * rank, rank), :] = spread_out.astype(B16)
    for kind, (wide, rows) in enumerate(((back, tokens), (low, grads))):
        term = SCALE * dot(wide[...], rows[...], 1, 0)

        @pl.when(table[0] == kind)
        def _(term=term):
            kept[...] = term

        @pl.when(table[0] != kind)
        def _(term=term):
            sent[...] = term.astype(B16)


def maps_of(table, rank, slots, parts, relative, tokens, grads):
    rows, width = tokens.shape
    arrays = [*parts, relative, tokens, grads]
    outs = [
        jax.ShapeDtypeStruct((slots * rank, rows), B16),
        jax.ShapeDtypeStruct((slots * rank, rows), B16),
        jax.ShapeDtypeStruct((slots * rank, width), F32),
        jax.ShapeDtypeStruct((slots * rank, width), B16),
    ]
    body = functools.partial(maps_body, rank, len(parts))
    specs = [whole(v) for v in arrays]
    return call(body, table, (1,), arrays, specs, outs, [whole(v) for v in outs], [], 0)


def lora_body(table, low, up, back, down, out, into):
    out[...] = (SCALE * dot(low[...], up[...], 0, 0)).astype(B16)
    into[...] = (SCALE * dot(back[...], down[...], 0, 0)).astype(B16)


def lora_of(low, up, back, down):
    rows, width = low.shape[1], up.shape[1]
    arrays = [low, up, back, down]
    out = jax.ShapeDtypeStruct((rows, width), B16)
    specs = [whole(v) for v in arrays]
    table = jnp.zeros((1,), jnp.int32)
    return call(lora_body, table, (1,), arrays, specs, [out, out], [whole(out)] * 2, [], 0)


def finish_body(table, here, live, out_lora, term, in_lora, ends, there, there_end, theirs, theirs_end, kept, other, query, token_grad, down, up):
    for i, (mine, sums) in enumerate(((there, theirs), (there_end, theirs_end))):

        @pl.when(pl.program_id(0) == i)
        def _(mine=mine, sums=sums):
            total = here[...] + mine[...].astype(F32) + out_lora[...].astype(F32)
            query[...] = jnp.where(live[...] > 0, total, 0.0).astype(B16)
            total = term[...].astype(F32) + in_lora[...].astype(F32) + ends[...].astype(F32)
            token_grad[...] = (total + sums[...].astype(F32)).astype(B16)

    @pl.when((pl.program_id(0) == 0) & (table[0] == 0))
    def _():
        down[...] = kept[...]
        up[...] = other[...]

    @pl.when((pl.program_id(0) == 0) & (table[0] != 0))
    def _():
        down[...] = other[...]
        up[...] = kept[...]


def finish(core, here, live, out_lora, term, in_lora, ends, *rest):
    rows, width = here.shape
    kept = rest[-1]
    spec = pl.BlockSpec((rows // 2, width), lambda i, t: (i, 0))
    thin = pl.BlockSpec((rows // 2, 1), lambda i, t: (i, 0))
    out = jax.ShapeDtypeStruct((rows, width), B16)
    small = jax.ShapeDtypeStruct(kept.shape, F32)
    return call(
        finish_body,
        core[None],
        (2,),
        [here, live, out_lora, term, in_lora, ends, *rest],
        [spec, thin, spec, spec, spec, spec] + [whole(v) for v in rest],
        [out, out, small, small],
        [spec, spec, whole(small), whole(small)],
        [],
        0,
    )


def add_body(table, a, b, out):
    out[...] = (a[...].astype(F32) + b[...].astype(F32)).astype(B16)


def add(a, b):
    rows, width = a.shape
    spec = pl.BlockSpec((rows // 2, width), lambda i, t: (i, 0))
    out = jax.ShapeDtypeStruct(a.shape, B16)
    table = jnp.zeros((1,), jnp.int32)
    return call(add_body, table, (2,), [a, b], [spec] * 2, out, spec, [], 0)


def shards_line(tokens, weight, down_maps, up_maps, counts, slot_of, cotangent):
    rows, width = tokens.shape
    held, _, rank = down_maps.shape
    n = lax.axis_size("tensor")
    slots = held * 2
    z = lax.axis_index("tensor")
    owner = lax.axis_index("tenant")
    core = lax.axis_index("dp")
    swap = [(0, 1), (1, 0)]
    ahead = jnp.where(core == 0, z, n - 1 - z)
    line_pairs = []
    for i in range(n - 1):
        line_pairs += [(2 * i, 2 * i + 2), (2 * i + 3, 2 * i + 1)]

    def along(value):
        return lax.ppermute(value, ("tensor", "dp"), line_pairs)

    def other_tenant(value):
        return lax.ppermute(value, "tenant", swap)

    def other_core(value):
        return lax.ppermute(value, "dp", swap)

    def numbers(*values):
        return jnp.stack([v.astype(jnp.int32) for v in values])

    chunk_of = [z]
    choice_of = [jnp.zeros((), jnp.int32)]
    kinds_of = [None]
    for choices in arrival_plan(n):
        kinds = sorted({(t, d == c) for t, d, _ in choices for c in range(2)})
        chunk = choice = jnp.zeros((), jnp.int32)
        for at, (t, direction, source) in enumerate(choices):
            chunk = jnp.where(z == at, source, chunk)
            for c in range(2):
                here = (z == at) & (core == c)
                choice = jnp.where(here, kinds.index((t, direction == c)), choice)
        chunk_of.append(chunk)
        choice_of.append(choice)
        kinds_of.append(kinds)

    st = {}

    def fence():
        names = [name for name in st if name not in FREE]
        st.update(zip(names, lax.optimization_barrier([st[name] for name in names])))

    def hop_of(k):
        t, side = k // 2 + 1, k % 2
        chunk = jnp.clip(n + ahead + 1 - t, 0, n - 1)
        chunk = jnp.where(core == 0, chunk, n - 1 - chunk)
        sums = (ahead < n - 1) & (ahead < t - 1)
        table = numbers(chunk, sums, 1 - core)
        grads = st["their_grads" if side else "grads"]
        st["sent"], st["share"] = hop(table, grads, st["weight"], st["line", t - 1, side])

    def offers_of(step):
        if step == 0:
            return [[st["tokens"]], [st["their_tokens"]]]
        kinds = kinds_of[step]
        return [
            [st["line", t, s] if mine else st["shared", t, 1 - s] for t, mine in kinds]
            for s in range(2)
        ]

    def piece_of(step, extra=()):
        table = numbers(choice_of[step], core)
        both = st["grads"], st["their_grads"]
        st["mix", step], *st["kept"] = piece(table, *offers_of(step), *both, extra)

    def sum_of(step):
        at = (2 * chunk_of[step] + core)[None]
        pair = st.pop(("mix", step)), st.pop(("x", step))
        shape = n * width, width
        st["wg"], st["ours", step] = place_sum(at, *pair, st.get("wg"), shape, width // 2)

    def place_of(step, theirs):
        at = (2 * chunk_of[step] + 1 - core)[None]
        st["wg"] = place(at, theirs, st["wg"], (n * width, width))

    st["weight"], st["tokens"], st["z"] = weight, tokens, z
    line = along(tokens)
    st["their_tokens"] = other_core(tokens)
    theirs = other_core(cotangent)
    mine = jnp.stack([jnp.swapaxes(down_maps, 1, 2), up_maps]).reshape(2, -1, width)
    st["fetched"] = other_tenant(lax.dynamic_index_in_dim(mine, core, 0, keepdims=False))
    st["mine"] = mine
    row_ids = (owner * 2 + core) * rows + jnp.arange(rows, dtype=jnp.int32)
    tenant, live = layout(counts, row_ids)
    relative = lax.rem(lookup(slot_of, tenant) + (2 - owner) * held, slots)
    st["relative"] = relative[None, :]
    st["live"] = live.astype(F32)[:, None]
    their_live = layout(counts, row_ids + (1 - 2 * core) * rows)[1]
    st["grads"] = jnp.where(live[:, None], cotangent, jnp.zeros_like(cotangent))
    st["their_grads"] = jnp.where(their_live[:, None], theirs, jnp.zeros_like(cotangent))
    fence()

    coming = along(st["their_tokens"])
    piece_of(0)
    swapped = other_tenant(st["mix", 0])
    shared = other_core(st["fetched"])
    names = ("relative", "tokens", "grads")
    st["down"], st["up"], st["part"] = ranks_of(
        core[None], rank, st.pop("mine"), st.pop("fetched"), shared, *[st[v] for v in names]
    )
    st["line", 1, 0] = line
    line = coming
    fence()

    wg_share = None
    for k in range(2, 2 * n + 1):
        t, side, step = k // 2 + 1, k % 2, k // 2
        last = k == 2 * n
        if not last:
            hop_of(k)
        if k == 2:
            for d in range(1, n):
                pairs = [(i, (i + d) % n) for i in range(n)]
                st["part", d] = lax.ppermute(st["part"], "tensor", pairs)
        fence()
        if not last:
            coming = along(st.pop("sent"))
            st["shared", t - 1, side] = other_core(st.pop("share"))
        if side == 1:
            extra = ()
            if step == 2:
                extra = st.pop("maps"), st.pop("came")
            if step == n - 1:
                kept = st.pop("kept")
            piece_of(step, extra)
            if step == n - 1:
                st["kept"] = kept[:1]
                st["maps_x"] = other_tenant(kept[1])
            st["x", step - 1] = swapped
            fence()
            swapped = other_tenant(st["mix", step])
            sum_of(step - 1)
        elif 4 <= k < 2 * n:
            wg_share = other_core(st["ours", step - 2])
        if k >= 6 and side == 0:
            place_of(step - 3, st.pop("theirs"))
        if k == 2:
            st["low"], st["back"], st["maps"], st["for_sibling"] = maps_of(
                core[None],
                rank,
                slots,
                [st.pop("part")] + [st.pop(("part", d)) for d in range(1, n)],
                *[st[v] for v in names],
            )
            st["came"] = other_core(st.pop("for_sibling"))
        if k == 4:
            st["term"] = term_of(st["z"][None], st["grads"], st["weight"])
        if k == 6:
            maps = [st.pop(v) for v in ("low", "up", "back", "down")]
            st["lora_out"], st["lora_in"] = lora_of(*maps)
        if last:
            offers = [offers_of(s) for s in range(n)]
            table = numbers(core, *chunk_of, *choice_of)
            st["query_here"], *st["query_there"] = query_parts(table, offers, st["weight"])
        st["line", (k - 1) // 2 + 1, 1 - side] = line
        line = coming
        if side == 1 and wg_share is not None:
            st["theirs"] = wg_share
            wg_share = None
        fence()

    kept = st.pop("kept")[0] + st.pop("maps_x").astype(F32)
    other = other_core(kept)
    there = [other_core(v) for v in st.pop("query_there")]
    theirs = [other_core(v) for v in jnp.split(st["line", n, 1], 2)]
    sums = [st.pop(v) for v in ("query_here", "live", "lora_out", "term", "lora_in")]
    ends = st["line", n, 0]
    done = finish(core, *sums, ends, *there, *theirs, kept, other)
    st["query"], st["token_grad"], down_grad, up_grad = done
    st["down_grad"] = jnp.swapaxes(down_grad.reshape(held, rank, width), 1, 2)
    st["up_grad"] = up_grad.reshape(held, rank, width)
    fence()
    st["x", n - 1] = swapped
    fence()
    st["ours", n - 1] = add(st["mix", n - 1], st["x", n - 1])
    earlier = other_core(st["ours", n - 2])
    theirs = other_core(st["ours", n - 1])
    shape = n * width, width
    mine_at = (2 * chunk_of[n - 1] + core)[None]
    st["wg"] = place(mine_at, st["ours", n - 1], st["wg"], shape)
    place_of(n - 2, earlier)
    place_of(n - 1, theirs)
    return st["query"], st["token_grad"], st["wg"], st["down_grad"], st["up_grad"]


def solution(mesh):
    placed = (
        P(("groups", "tenant", "dp"), "tensor"),
        P(None, "tensor"),
        P("tenant", "tensor", None),
        P("tenant", None, "tensor"),
        P("groups"),
        P(),
        P(("groups", "tenant", "dp"), "tensor"),
    )
    short = mesh.shape["tensor"] == 4
    paired = mesh.shape["tenant"] == 2 and mesh.shape["dp"] == 2
    return jax.shard_map(
        shards_line if short and paired else shards_general,
        mesh=mesh,
        in_specs=placed,
        out_specs=(
            P(("groups", "tenant", "dp"), "tensor"),
            P(("groups", "tenant", "dp"), "tensor"),
            P("groups", "tensor"),
            P(("groups", "tenant"), "tensor", None),
            P(("groups", "tenant"), None, "tensor"),
        ),
        check_vma=False,
    )
```

```python
import functools

import jax
import jax.numpy as jnp
from jax import lax
from jax.experimental import pallas as pl
from jax.experimental.pallas import tpu as pltpu
from jax.sharding import PartitionSpec as P

BLOCK_ROWS = 128
SCALE = 2.0
F32 = jnp.float32
B16 = jnp.bfloat16


def dot(a, b, ca, cb):
    return lax.dot_general(a, b, (((ca,), (cb,)), ((), ())), preferred_element_type=F32)


def lookup(source, position):
    match_mask = position[..., None] == jnp.arange(source.shape[0], dtype=jnp.int32)
    return jnp.sum(jnp.where(match_mask, source, 0), axis=-1)


def layout(tenant_row_counts, row_ids):
    block_count = (tenant_row_counts + BLOCK_ROWS - 1) // BLOCK_ROWS
    segment_offset = jnp.cumsum(block_count) - block_count
    block_ids = row_ids // BLOCK_ROWS
    tenant_of = (
        jnp.sum((segment_offset[None, :] <= block_ids[:, None]).astype(jnp.int32), axis=1) - 1
    )
    offset = row_ids - BLOCK_ROWS * lookup(segment_offset, tenant_of)
    return tenant_of, offset < lookup(tenant_row_counts, tenant_of)


def rank_partials(maps, rows, mask, slots):
    every = dot(maps, rows, 1, 1)
    every = every.reshape(slots, -1, rows.shape[0])
    return jnp.sum(jnp.where(mask[:, None, :], every, 0.0), axis=0)


def spread(values, mask):
    wide = jnp.where(mask[:, None, :], values[None], jnp.zeros((), values.dtype))
    return wide.reshape(-1, values.shape[-1])


def shards_general(tokens, weight, down_maps, up_maps, counts, slot_of, cotangent):
    rows, width = tokens.shape
    held, _, rank = down_maps.shape
    slots = held * lax.axis_size("tenant")
    owner = lax.axis_index("tenant")
    row_ids = lax.axis_index(("tenant", "dp")) * rows + jnp.arange(rows, dtype=jnp.int32)
    tenant, live = layout(counts, row_ids)
    slot = lookup(slot_of, tenant)
    mask = slot[None, :] == jnp.arange(slots, dtype=jnp.int32)[:, None]
    grads = jnp.where(live[:, None], cotangent, jnp.zeros_like(cotangent))
    kept = jnp.where(live[:, None], tokens, jnp.zeros_like(tokens))
    down = lax.all_gather(jnp.swapaxes(down_maps, 1, 2), "tenant", axis=0, tiled=True)
    up = lax.all_gather(up_maps, "tenant", axis=0, tiled=True)
    down, up = down.reshape(-1, width), up.reshape(-1, width)
    gathered = lax.all_gather(kept, "tensor", axis=1, tiled=True)
    part = jnp.stack(
        [rank_partials(down, kept, mask, slots), rank_partials(up, grads, mask, slots)]
    )
    low, back = lax.psum(part.astype(B16), "tensor")
    low, back = spread(low, mask), spread(back, mask)
    base = dot(gathered, weight, 1, 0)
    query = (base + (SCALE * dot(low, up, 0, 0)).astype(B16).astype(F32)).astype(B16)
    term = dot(grads, weight, 1, 1).astype(B16)
    summed = lax.psum_scatter(term, "tensor", scatter_dimension=1, tiled=True).astype(F32)
    lora = (SCALE * dot(back, down, 0, 0)).astype(B16).astype(F32)
    token_grad = jnp.where(live[:, None], summed + lora, 0.0).astype(B16)
    axes = ("tenant", "dp")
    weight_grad = lax.psum(dot(gathered, grads, 0, 0).astype(B16), axes)
    maps = jnp.stack([SCALE * dot(back, kept, 1, 0), SCALE * dot(low, grads, 1, 0)])
    maps = lax.psum(maps.astype(B16), axes).astype(F32).reshape(2, slots, rank, width)
    maps = lax.dynamic_slice_in_dim(maps, owner * held, held, 1)
    return query, token_grad, weight_grad, jnp.swapaxes(maps[0], 1, 2), maps[1]


def arrival_plan(n):
    plan = [[] for _ in range(n - 1)]
    for z in range(n):
        seen = []
        for t in range(1, n):
            if z - t >= 0:
                seen.append((t, 0, z - t))
            if z + t < n:
                seen.append((t, 1, z + t))
        for step, entry in enumerate(seen):
            plan[step].append(entry)
    return plan


def whole(array):
    return pl.BlockSpec(array.shape, lambda *_: (0,) * array.ndim)


def call(body, table, grid, arrays, specs, outs, out_specs, scratch, flops, aliases=None, pinned=(), limit=48):
    arrays = list(arrays)
    for at in pinned:
        arrays[at] = pltpu.with_memory_space_constraint(arrays[at], pltpu.HBM)
    return pl.pallas_call(
        body,
        grid_spec=pltpu.PrefetchScalarGridSpec(
            num_scalar_prefetch=1,
            grid=grid,
            in_specs=specs,
            out_specs=out_specs,
            scratch_shapes=scratch,
        ),
        out_shape=outs,
        input_output_aliases=aliases or {},
        compiler_params=pltpu.CompilerParams(vmem_limit_bytes=limit * 1024 * 1024),
        cost_estimate=pl.CostEstimate(flops=1, bytes_accessed=1, transcendentals=0),
    )(table, *arrays)


FREE = ()
HOP_STEPS = 2


def hop_body(table, grads, weight, came, goes, share):
    @pl.when(pl.program_id(0) == table[2])
    def _():
        share[...] = came[...]

    @pl.when(table[1] == 0)
    def _():
        goes[...] = came[...]

    @pl.when(table[1] != 0)
    def _():
        term = dot(grads[...], weight[...], 1, 1)
        goes[...] = (term + came[...].astype(F32)).astype(B16)


def hop(table, grads, weight, came):
    rows, width = came.shape
    half, step = width // 2, width // HOP_STEPS
    cols = pl.BlockSpec((rows, step), lambda j, t: (0, j))
    return call(
        hop_body,
        table,
        (HOP_STEPS,),
        [grads, weight, came],
        [
            whole(grads),
            pl.BlockSpec((step, width), lambda j, t: (HOP_STEPS * t[0] + j, 0)),
            cols,
        ],
        [jax.ShapeDtypeStruct((rows, width), B16), jax.ShapeDtypeStruct((rows, half), B16)],
        [cols, pl.BlockSpec((rows, half), lambda j, t: (0, 0))],
        [],
        0,
    )


def start_chosen(choice, offers, core, target, done):
    rows, half = target.shape
    for at, offer in enumerate(offers):

        @pl.when(choice == at)
        def _(offer=offer):
            source = offer
            if offer.shape[1] != half:
                source = offer.at[:, pl.ds(pl.multiple_of(core * half, half), half)]
            pltpu.make_async_copy(source, target, done).start()


def wait_chosen(target, done):
    pltpu.make_async_copy(target, target, done).wait()


def piece_body(count, extra, table, *refs):
    ours, theirs = refs[:count], refs[count : 2 * count]
    grads, their_grads = refs[2 * count : 2 * count + 2]
    rest = refs[2 * count + 2 :]
    out, a, b, done = rest[2 * extra], *rest[-3:]
    half = a.shape[1]

    @pl.when(pl.program_id(0) == 0)
    def _():
        start_chosen(table[0], ours, table[1], a, done.at[0])
        start_chosen(table[0], theirs, table[1], b, done.at[1])
        wait_chosen(a, done.at[0])
        wait_chosen(b, done.at[1])

    mix = dot(a[...], grads[...], 0, 0) + dot(b[...], their_grads[...], 0, 0)
    out[...] = mix.astype(B16)
    if extra:
        maps, came, kept, sent = rest[0], rest[1], rest[3], rest[4]
        split = kept.shape[0]
        total = maps[...] + came[...].astype(F32)
        kept[...] = total[:split]
        sent[...] = total[split:].astype(B16)


def piece(table, ours, theirs, grads, their_grads, extra=()):
    rows, width = grads.shape
    half = width // 2

    def cols(count):
        return pl.BlockSpec((count, width // 2), lambda j, t: (0, j))

    split = extra[0].shape[0] // 2 if extra else 0
    outs = [jax.ShapeDtypeStruct((half, width), B16)]
    if extra:
        outs.append(jax.ShapeDtypeStruct((split, width), F32))
        outs.append(jax.ShapeDtypeStruct((split, width), B16))
    return call(
        functools.partial(piece_body, len(ours), 1 if extra else 0),
        table,
        (2,),
        [*ours, *theirs, grads, their_grads, *extra],
        [pl.BlockSpec(memory_space=pltpu.HBM)] * (2 * len(ours))
        + [cols(rows), cols(rows)]
        + [cols(2 * split)] * len(extra),
        outs,
        [cols(v.shape[0]) for v in outs],
        [pltpu.VMEM((rows, half), B16)] * 2 + [pltpu.SemaphoreType.DMA((2,))],
        0,
        pinned=range(2 * len(ours)),
    )


def query_body(groups, n, half, table, *refs):
    offers, blocks = refs[: -6 - n], refs[-6 - n : -6]
    own_out, other_out, other_end, rows_in, weight_in, done = refs[-6:]
    rows = own_out.shape[0]

    @pl.when(pl.program_id(0) == 0)
    def _():
        at = 0
        waits = []
        for step, count in enumerate(groups):
            start = pl.multiple_of(table[1 + step] * half, half)
            for side in range(2):
                here = offers[at : at + count]
                at += count
                target = rows_in.at[pl.ds(side * rows, rows), pl.ds(start, half)]
                sem = done.at[2 * step + side]
                start_chosen(table[1 + n + step], here, table[0], target, sem)
                waits.append((target, sem))
        for target, sem in waits:
            wait_chosen(target, sem)

    for chunk in range(n):
        weight_in[pl.ds(chunk * half, half), :] = blocks[chunk][...]
    own_out[...] = dot(rows_in[pl.ds(0, rows), :], weight_in[...], 1, 0)
    other = dot(rows_in[pl.ds(rows, rows), :], weight_in[...], 1, 0).astype(B16)
    other_out[...] = other[: rows // 2]
    other_end[...] = other[rows // 2 :]


def query_parts(table, offers, weight):
    n = len(offers)
    rows, width = offers[0][0][0].shape[0], weight.shape[1]
    half = cols = width // 2
    flat = [v for pair in offers for side in pair for v in side]

    def block(chunk):
        return pl.BlockSpec((half, cols), lambda j, t: (2 * chunk + t[0], j))

    out = pl.BlockSpec((rows, cols), lambda j, t: (0, j))
    part = pl.BlockSpec((rows // 2, cols), lambda j, t: (0, j))
    return call(
        functools.partial(query_body, [len(pair[0]) for pair in offers], n, half),
        table,
        (2,),
        [*flat] + [weight] * n,
        [pl.BlockSpec(memory_space=pltpu.HBM)] * len(flat) + [block(c) for c in range(n)],
        [
            kept_in_hbm(jax.ShapeDtypeStruct((rows, width), F32)),
            jax.ShapeDtypeStruct((rows // 2, width), B16),
            jax.ShapeDtypeStruct((rows // 2, width), B16),
        ],
        [out, part, part],
        [
            pltpu.VMEM((2 * rows, n * half), B16),
            pltpu.VMEM((n * half, cols), B16),
            pltpu.SemaphoreType.DMA((2 * n,)),
        ],
        0,
        pinned=range(len(flat)),
        limit=28,
    )


def term_body(table, grads, weight, out):
    out[...] = dot(grads[...], weight[...], 1, 1).astype(B16)


def term_of(table, grads, weight):
    rows, width = grads.shape
    half = width // 2
    return call(
        term_body,
        table,
        (2,),
        [grads, weight],
        [whole(grads), pl.BlockSpec((half, width), lambda j, t: (2 * t[0] + j, 0))],
        kept_in_hbm(jax.ShapeDtypeStruct((rows, width), B16)),
        pl.BlockSpec((rows, half), lambda j, t: (0, j)),
        [],
        2 * rows * width * width,
    )


def into_target(value, target, shape, at, body, extra, outs, steps):
    rows, width = shape[2], shape[1]
    block = rows // steps
    spec = pl.BlockSpec((block, width), lambda i, t: (i, 0))
    arrays, specs, aliases = [value, *extra], [spec] * (1 + len(extra)), {}
    if target is not None:
        aliases = {1 + len(arrays): 0}
        arrays.append(target)
        specs.append(pl.BlockSpec(memory_space=pl.ANY))
    where = pl.BlockSpec((block, width), lambda i, t: (steps * t[0] + i, 0))
    return call(
        body,
        at,
        (steps,),
        arrays,
        specs,
        [jax.ShapeDtypeStruct(shape[:2], B16)] + [jax.ShapeDtypeStruct((rows, width), B16)] * outs,
        [where] + [spec] * outs,
        [],
        0,
        aliases,
    )


def place_body(table, value, *refs):
    refs[-1][...] = value[...]


def place(at, value, target, shape):
    return into_target(value, target, (*shape, value.shape[0]), at, place_body, (), 0, 2)[0]


def sum_body(table, a, b, *refs):
    total = (a[...].astype(F32) + b[...].astype(F32)).astype(B16)
    refs[-2][...] = total
    refs[-1][...] = total


def place_sum(at, a, b, target, shape, rows):
    return into_target(a, target, (*shape, rows), at, sum_body, (b,), 1, 2)


def ranks_body(rank, table, mine, fetched, shared, relative, tokens, grads, down, up, part):
    split = mine.shape[1]
    down[pl.ds(0, split), :] = mine[0]
    up[pl.ds(0, split), :] = mine[1]

    @pl.when(table[0] == 0)
    def _():
        down[pl.ds(split, split), :] = fetched[...]
        up[pl.ds(split, split), :] = shared[...]

    @pl.when(table[0] != 0)
    def _():
        down[pl.ds(split, split), :] = shared[...]
        up[pl.ds(split, split), :] = fetched[...]

    for kind, (maps, rows) in enumerate(((down, tokens), (up, grads))):
        every = dot(maps[...], rows[...], 1, 1)
        total = None
        for slot in range(2 * split // rank):
            own = jnp.where(relative[...] == slot, every[slot * rank : (slot + 1) * rank], 0.0)
            total = own if total is None else total + own
        part[pl.ds(kind * rank, rank), :] = total.astype(B16)


def ranks_of(table, rank, mine, fetched, shared, relative, tokens, grads):
    rows, width = tokens.shape
    arrays = [mine, fetched, shared, relative, tokens, grads]
    outs = [
        jax.ShapeDtypeStruct((2 * mine.shape[1], width), B16),
        jax.ShapeDtypeStruct((2 * mine.shape[1], width), B16),
        jax.ShapeDtypeStruct((2 * rank, rows), B16),
    ]
    body = functools.partial(ranks_body, rank)
    specs = [whole(v) for v in arrays]
    return call(body, table, (1,), arrays, specs, [kept_in_hbm(v) for v in outs], [whole(v) for v in outs], [], 0)


def maps_body(rank, count, table, *refs):
    relative, tokens, grads, low, back, kept, sent = refs[count:]
    total = refs[0][...].astype(F32)
    for part in refs[1:count]:
        total += part[...].astype(F32)
    total = total.astype(B16).astype(F32)
    for kind, wide in enumerate((low, back)):
        own = total[kind * rank : (kind + 1) * rank]
        for slot in range(wide.shape[0] // rank):
            spread_out = jnp.where(relative[...] == slot, own, 0.0)
            wide[pl.ds(slot * rank, rank), :] = spread_out.astype(B16)
    for kind, (wide, rows) in enumerate(((back, tokens), (low, grads))):
        term = SCALE * dot(wide[...], rows[...], 1, 0)

        @pl.when(table[0] == kind)
        def _(term=term):
            kept[...] = term

        @pl.when(table[0] != kind)
        def _(term=term):
            sent[...] = term.astype(B16)


def maps_of(table, rank, slots, parts, relative, tokens, grads):
    rows, width = tokens.shape
    arrays = [*parts, relative, tokens, grads]
    outs = [
        jax.ShapeDtypeStruct((slots * rank, rows), B16),
        jax.ShapeDtypeStruct((slots * rank, rows), B16),
        jax.ShapeDtypeStruct((slots * rank, width), F32),
        jax.ShapeDtypeStruct((slots * rank, width), B16),
    ]
    body = functools.partial(maps_body, rank, len(parts))
    specs = [whole(v) for v in arrays]
    return call(body, table, (1,), arrays, specs, [kept_in_hbm(v) for v in outs], [whole(v) for v in outs], [], 0)


def lora_body(table, low, up, back, down, out, into):
    out[...] = (SCALE * dot(low[...], up[...], 0, 0)).astype(B16)
    into[...] = (SCALE * dot(back[...], down[...], 0, 0)).astype(B16)


def lora_of(low, up, back, down):
    rows, width = low.shape[1], up.shape[1]
    arrays = [low, up, back, down]
    out = jax.ShapeDtypeStruct((rows, width), B16)
    specs = [whole(v) for v in arrays]
    table = jnp.zeros((1,), jnp.int32)
    return call(lora_body, table, (1,), arrays, specs, [kept_in_hbm(out)] * 2, [whole(out)] * 2, [], 0)


def finish_body(table, here, live, out_lora, term, in_lora, ends, there, there_end, theirs, theirs_end, kept, other, query, token_grad, down, up):
    for i, (mine, sums) in enumerate(((there, theirs), (there_end, theirs_end))):

        @pl.when(pl.program_id(0) == i)
        def _(mine=mine, sums=sums):
            total = here[...] + mine[...].astype(F32) + out_lora[...].astype(F32)
            query[...] = jnp.where(live[...] > 0, total, 0.0).astype(B16)
            total = term[...].astype(F32) + in_lora[...].astype(F32) + ends[...].astype(F32)
            token_grad[...] = (total + sums[...].astype(F32)).astype(B16)

    @pl.when((pl.program_id(0) == 0) & (table[0] == 0))
    def _():
        down[...] = kept[...]
        up[...] = other[...]

    @pl.when((pl.program_id(0) == 0) & (table[0] != 0))
    def _():
        down[...] = other[...]
        up[...] = kept[...]


def finish(core, here, live, out_lora, term, in_lora, ends, *rest):
    rows, width = here.shape
    kept = rest[-1]
    spec = pl.BlockSpec((rows // 2, width), lambda i, t: (i, 0))
    thin = pl.BlockSpec((rows // 2, 1), lambda i, t: (i, 0))
    out = jax.ShapeDtypeStruct((rows, width), B16)
    small = jax.ShapeDtypeStruct(kept.shape, F32)
    return call(
        finish_body,
        core[None],
        (2,),
        [here, live, out_lora, term, in_lora, ends, *rest],
        [spec, thin, spec, spec, spec, spec] + [whole(v) for v in rest],
        [out, out, small, small],
        [spec, spec, whole(small), whole(small)],
        [],
        0,
    )


def add_body(table, a, b, out):
    out[...] = (a[...].astype(F32) + b[...].astype(F32)).astype(B16)


def add(a, b):
    rows, width = a.shape
    spec = pl.BlockSpec((rows // 2, width), lambda i, t: (i, 0))
    out = jax.ShapeDtypeStruct(a.shape, B16)
    table = jnp.zeros((1,), jnp.int32)
    return call(add_body, table, (2,), [a, b], [spec] * 2, out, spec, [], 0)


def mask_body(tenants, slots, table, mine, theirs, grads, their_grads, slot_rows, live):
    blocks = mine.shape[0] // BLOCK_ROWS
    row = lax.broadcasted_iota(jnp.int32, (BLOCK_ROWS, 1), 0)
    for side, (rows_in, rows_out) in enumerate(((mine, grads), (theirs, their_grads))):
        for b in range(blocks):
            block = table[2 * tenants + side] + b
            start = jnp.int32(0)
            left = slot = jnp.int32(0)
            for t in range(tenants):
                here = start <= block
                left = jnp.where(here, table[t] - BLOCK_ROWS * (block - start), left)
                slot = jnp.where(here, table[tenants + t], slot)
                start = start + (table[t] + BLOCK_ROWS - 1) // BLOCK_ROWS
            at = pl.ds(b * BLOCK_ROWS, BLOCK_ROWS)
            alive = row < left
            rows_out[at, :] = jnp.where(alive, rows_in[at, :].astype(F32), 0.0).astype(B16)
            if side == 0:
                live[at, :] = jnp.where(alive, 1.0, 0.0)
                placed = lax.rem(slot + table[2 * tenants + 2], slots)
                slot_rows[:, at] = jnp.full((1, BLOCK_ROWS), placed, jnp.int32)


def masked(table, tenants, slots, mine, theirs):
    rows, width = mine.shape
    outs = [
        jax.ShapeDtypeStruct((rows, width), B16),
        jax.ShapeDtypeStruct((rows, width), B16),
        jax.ShapeDtypeStruct((1, rows), jnp.int32),
        jax.ShapeDtypeStruct((rows, 1), F32),
    ]
    body = functools.partial(mask_body, tenants, slots)
    specs = [whole(mine), whole(theirs)]
    return call(body, table, (1,), [mine, theirs], specs, outs, [whole(v) for v in outs], [], 0)


def kept_in_hbm(shape):
    return pltpu.HBM(shape.shape, shape.dtype)


def shards_line(tokens, weight, down_maps, up_maps, counts, slot_of, cotangent):
    rows, width = tokens.shape
    held, _, rank = down_maps.shape
    n = lax.axis_size("tensor")
    slots = held * 2
    z = lax.axis_index("tensor")
    owner = lax.axis_index("tenant")
    core = lax.axis_index("dp")
    swap = [(0, 1), (1, 0)]
    ahead = jnp.where(core == 0, z, n - 1 - z)
    line_pairs = []
    for i in range(n - 1):
        line_pairs += [(2 * i, 2 * i + 2), (2 * i + 3, 2 * i + 1)]

    def along(value):
        return lax.ppermute(value, ("tensor", "dp"), line_pairs)

    def other_tenant(value):
        return lax.ppermute(value, "tenant", swap)

    def other_core(value):
        return lax.ppermute(value, "dp", swap)

    def numbers(*values):
        return jnp.stack([v.astype(jnp.int32) for v in values])

    chunk_of = [z]
    choice_of = [jnp.zeros((), jnp.int32)]
    kinds_of = [None]
    for choices in arrival_plan(n):
        kinds = sorted({(t, d == c) for t, d, _ in choices for c in range(2)})
        chunk = choice = jnp.zeros((), jnp.int32)
        for at, (t, direction, source) in enumerate(choices):
            chunk = jnp.where(z == at, source, chunk)
            for c in range(2):
                here = (z == at) & (core == c)
                choice = jnp.where(here, kinds.index((t, direction == c)), choice)
        chunk_of.append(chunk)
        choice_of.append(choice)
        kinds_of.append(kinds)

    st = {}

    def fence():
        names = [name for name in st if name not in FREE]
        st.update(zip(names, lax.optimization_barrier([st[name] for name in names])))

    def hop_of(k):
        t, side = k // 2 + 1, k % 2
        chunk = jnp.clip(n + ahead + 1 - t, 0, n - 1)
        chunk = jnp.where(core == 0, chunk, n - 1 - chunk)
        sums = (ahead < n - 1) & (ahead < t - 1)
        table = numbers(chunk, sums, 1 - core)
        grads = st["their_grads" if side else "grads"]
        st["sent"], st["share"] = hop(table, grads, st["weight"], st["line", t - 1, side])

    def offers_of(step):
        if step == 0:
            return [[st["tokens"]], [st["their_tokens"]]]
        kinds = kinds_of[step]
        return [
            [st["line", t, s] if mine else st["shared", t, 1 - s] for t, mine in kinds]
            for s in range(2)
        ]

    def piece_of(step, extra=()):
        table = numbers(choice_of[step], core)
        both = st["grads"], st["their_grads"]
        st["mix", step], *st["kept"] = piece(table, *offers_of(step), *both, extra)

    def sum_of(step):
        at = (2 * chunk_of[step] + core)[None]
        pair = st.pop(("mix", step)), st.pop(("x", step))
        shape = n * width, width
        st["wg"], st["ours", step] = place_sum(at, *pair, st.get("wg"), shape, width // 2)

    def place_of(step, theirs):
        at = (2 * chunk_of[step] + 1 - core)[None]
        st["wg"] = place(at, theirs, st["wg"], (n * width, width))

    st["weight"], st["tokens"], st["z"] = weight, tokens, z
    line = along(tokens)
    st["their_tokens"] = other_core(tokens)
    theirs = other_core(cotangent)
    mine = jnp.stack([jnp.swapaxes(down_maps, 1, 2), up_maps]).reshape(2, -1, width)
    st["fetched"] = other_tenant(lax.dynamic_index_in_dim(mine, core, 0, keepdims=False))
    st["mine"] = mine
    blocks = rows // BLOCK_ROWS
    first = (owner * 2 + core) * blocks
    their_first = (owner * 2 + 1 - core) * blocks
    places = numbers(first, their_first, (2 - owner) * held)
    table = jnp.concatenate([counts, slot_of, places])
    st["grads"], st["their_grads"], st["relative"], st["live"] = masked(
        table, counts.shape[0], slots, cotangent, theirs
    )
    fence()

    coming = along(st["their_tokens"])
    piece_of(0)
    swapped = other_tenant(st["mix", 0])
    shared = other_core(st["fetched"])
    names = ("relative", "tokens", "grads")
    st["down"], st["up"], st["part"] = ranks_of(
        core[None], rank, st.pop("mine"), st.pop("fetched"), shared, *[st[v] for v in names]
    )
    st["line", 1, 0] = line
    line = coming
    fence()

    wg_share = None
    for k in range(2, 2 * n + 1):
        t, side, step = k // 2 + 1, k % 2, k // 2
        last = k == 2 * n
        if not last:
            hop_of(k)
        if k == 2:
            for d in range(1, n):
                pairs = [(i, (i + d) % n) for i in range(n)]
                st["part", d] = lax.ppermute(st["part"], "tensor", pairs)
        if k == 3:
            st["x", 0] = swapped
        if k == 6:
            st["maps_x"] = other_tenant(st["kept"].pop())
        fence()
        if k == 6:
            swapped = other_tenant(st["mix", 2])
        if not last:
            coming = along(st.pop("sent"))
            st["shared", t - 1, side] = other_core(st.pop("share"))
        if side == 1:
            extra = ()
            if step == 2:
                extra = st.pop("maps"), st.pop("came")
            if step == n - 1:
                kept = st.pop("kept")
            piece_of(step, extra)
            if step == n - 1:
                st["kept"] = kept[:1]
            if step > 1:
                st["x", step - 1] = swapped
            fence()
            if step != 2:
                swapped = other_tenant(st["mix", step])
            sum_of(step - 1)
        elif 4 <= k < 2 * n:
            wg_share = other_core(st["ours", step - 2])
        if k >= 6 and side == 0:
            place_of(step - 3, st.pop("theirs"))
        if k == 2:
            st["low"], st["back"], st["maps"], st["for_sibling"] = maps_of(
                core[None],
                rank,
                slots,
                [st.pop("part")] + [st.pop(("part", d)) for d in range(1, n)],
                *[st[v] for v in names],
            )
            st["came"] = other_core(st.pop("for_sibling"))
        if k == 4:
            st["term"] = term_of(st["z"][None], st["grads"], st["weight"])
        if k == 6:
            maps = [st.pop(v) for v in ("low", "up", "back", "down")]
            st["lora_out"], st["lora_in"] = lora_of(*maps)
        if last:
            offers = [offers_of(s) for s in range(n)]
            table = numbers(core, *chunk_of, *choice_of)
            st["query_here"], *st["query_there"] = query_parts(table, offers, st["weight"])
        st["line", (k - 1) // 2 + 1, 1 - side] = line
        line = coming
        if side == 1 and wg_share is not None:
            st["theirs"] = wg_share
            wg_share = None
        fence()

    kept = st.pop("kept")[0] + st.pop("maps_x").astype(F32)
    other = other_core(kept)
    there = [other_core(v) for v in st.pop("query_there")]
    theirs = [other_core(v) for v in jnp.split(st["line", n, 1], 2)]
    sums = [st.pop(v) for v in ("query_here", "live", "lora_out", "term", "lora_in")]
    ends = st["line", n, 0]
    done = finish(core, *sums, ends, *there, *theirs, kept, other)
    st["query"], st["token_grad"], down_grad, up_grad = done
    st["down_grad"] = jnp.swapaxes(down_grad.reshape(held, rank, width), 1, 2)
    st["up_grad"] = up_grad.reshape(held, rank, width)
    fence()
    st["x", n - 1] = swapped
    fence()
    st["ours", n - 1] = add(st["mix", n - 1], st["x", n - 1])
    earlier = other_core(st["ours", n - 2])
    theirs = other_core(st["ours", n - 1])
    shape = n * width, width
    mine_at = (2 * chunk_of[n - 1] + core)[None]
    st["wg"] = place(mine_at, st["ours", n - 1], st["wg"], shape)
    place_of(n - 2, earlier)
    place_of(n - 1, theirs)
    return st["query"], st["token_grad"], st["wg"], st["down_grad"], st["up_grad"]


def solution(mesh):
    placed = (
        P(("groups", "tenant", "dp"), "tensor"),
        P(None, "tensor"),
        P("tenant", "tensor", None),
        P("tenant", None, "tensor"),
        P("groups"),
        P(),
        P(("groups", "tenant", "dp"), "tensor"),
    )
    short = mesh.shape["tensor"] == 4
    paired = mesh.shape["tenant"] == 2 and mesh.shape["dp"] == 2
    return jax.shard_map(
        shards_line if short and paired else shards_general,
        mesh=mesh,
        in_specs=placed,
        out_specs=(
            P(("groups", "tenant", "dp"), "tensor"),
            P(("groups", "tenant", "dp"), "tensor"),
            P("groups", "tensor"),
            P(("groups", "tenant"), "tensor", None),
            P(("groups", "tenant"), None, "tensor"),
        ),
        check_vma=False,
    )
```

```python
import functools

import jax
import jax.numpy as jnp
from jax import lax
from jax.experimental import pallas as pl
from jax.experimental.pallas import tpu as pltpu
from jax.sharding import PartitionSpec as P

BLOCK_ROWS = 128
SCALE = 2.0
F32 = jnp.float32
B16 = jnp.bfloat16


def dot(a, b, ca, cb):
    return lax.dot_general(a, b, (((ca,), (cb,)), ((), ())), preferred_element_type=F32)


def lookup(source, position):
    match_mask = position[..., None] == jnp.arange(source.shape[0], dtype=jnp.int32)
    return jnp.sum(jnp.where(match_mask, source, 0), axis=-1)


def layout(tenant_row_counts, row_ids):
    block_count = (tenant_row_counts + BLOCK_ROWS - 1) // BLOCK_ROWS
    segment_offset = jnp.cumsum(block_count) - block_count
    block_ids = row_ids // BLOCK_ROWS
    tenant_of = (
        jnp.sum((segment_offset[None, :] <= block_ids[:, None]).astype(jnp.int32), axis=1) - 1
    )
    offset = row_ids - BLOCK_ROWS * lookup(segment_offset, tenant_of)
    return tenant_of, offset < lookup(tenant_row_counts, tenant_of)


def rank_partials(maps, rows, mask, slots):
    every = dot(maps, rows, 1, 1)
    every = every.reshape(slots, -1, rows.shape[0])
    return jnp.sum(jnp.where(mask[:, None, :], every, 0.0), axis=0)


def spread(values, mask):
    wide = jnp.where(mask[:, None, :], values[None], jnp.zeros((), values.dtype))
    return wide.reshape(-1, values.shape[-1])


def shards_general(tokens, weight, down_maps, up_maps, counts, slot_of, cotangent):
    rows, width = tokens.shape
    held, _, rank = down_maps.shape
    slots = held * lax.axis_size("tenant")
    owner = lax.axis_index("tenant")
    row_ids = lax.axis_index(("tenant", "dp")) * rows + jnp.arange(rows, dtype=jnp.int32)
    tenant, live = layout(counts, row_ids)
    slot = lookup(slot_of, tenant)
    mask = slot[None, :] == jnp.arange(slots, dtype=jnp.int32)[:, None]
    grads = jnp.where(live[:, None], cotangent, jnp.zeros_like(cotangent))
    kept = jnp.where(live[:, None], tokens, jnp.zeros_like(tokens))
    down = lax.all_gather(jnp.swapaxes(down_maps, 1, 2), "tenant", axis=0, tiled=True)
    up = lax.all_gather(up_maps, "tenant", axis=0, tiled=True)
    down, up = down.reshape(-1, width), up.reshape(-1, width)
    gathered = lax.all_gather(kept, "tensor", axis=1, tiled=True)
    part = jnp.stack(
        [rank_partials(down, kept, mask, slots), rank_partials(up, grads, mask, slots)]
    )
    low, back = lax.psum(part.astype(B16), "tensor")
    low, back = spread(low, mask), spread(back, mask)
    base = dot(gathered, weight, 1, 0)
    query = (base + (SCALE * dot(low, up, 0, 0)).astype(B16).astype(F32)).astype(B16)
    term = dot(grads, weight, 1, 1).astype(B16)
    summed = lax.psum_scatter(term, "tensor", scatter_dimension=1, tiled=True).astype(F32)
    lora = (SCALE * dot(back, down, 0, 0)).astype(B16).astype(F32)
    token_grad = jnp.where(live[:, None], summed + lora, 0.0).astype(B16)
    axes = ("tenant", "dp")
    weight_grad = lax.psum(dot(gathered, grads, 0, 0).astype(B16), axes)
    maps = jnp.stack([SCALE * dot(back, kept, 1, 0), SCALE * dot(low, grads, 1, 0)])
    maps = lax.psum(maps.astype(B16), axes).astype(F32).reshape(2, slots, rank, width)
    maps = lax.dynamic_slice_in_dim(maps, owner * held, held, 1)
    return query, token_grad, weight_grad, jnp.swapaxes(maps[0], 1, 2), maps[1]


def arrival_plan(n):
    plan = [[] for _ in range(n - 1)]
    for z in range(n):
        seen = []
        for t in range(1, n):
            if z - t >= 0:
                seen.append((t, 0, z - t))
            if z + t < n:
                seen.append((t, 1, z + t))
        for step, entry in enumerate(seen):
            plan[step].append(entry)
    return plan


def whole(array):
    return pl.BlockSpec(array.shape, lambda *_: (0,) * array.ndim)


def call(body, table, grid, arrays, specs, outs, out_specs, scratch, flops, aliases=None, pinned=(), limit=48):
    arrays = list(arrays)
    for at in pinned:
        arrays[at] = pltpu.with_memory_space_constraint(arrays[at], pltpu.HBM)
    return pl.pallas_call(
        body,
        grid_spec=pltpu.PrefetchScalarGridSpec(
            num_scalar_prefetch=1,
            grid=grid,
            in_specs=specs,
            out_specs=out_specs,
            scratch_shapes=scratch,
        ),
        out_shape=outs,
        input_output_aliases=aliases or {},
        compiler_params=pltpu.CompilerParams(vmem_limit_bytes=limit * 1024 * 1024),
        cost_estimate=pl.CostEstimate(flops=1, bytes_accessed=1, transcendentals=0),
    )(table, *arrays)


FREE = ()
HOP_STEPS = 2


def hop_body(table, grads, weight, came, goes, share):
    @pl.when(pl.program_id(0) == table[2])
    def _():
        share[...] = came[...]

    @pl.when(table[1] == 0)
    def _():
        goes[...] = came[...]

    @pl.when(table[1] != 0)
    def _():
        term = dot(grads[...], weight[...], 1, 1)
        goes[...] = (term + came[...].astype(F32)).astype(B16)


def hop(table, grads, weight, came):
    rows, width = came.shape
    half, step = width // 2, width // HOP_STEPS
    cols = pl.BlockSpec((rows, step), lambda j, t: (0, j))
    return call(
        hop_body,
        table,
        (HOP_STEPS,),
        [grads, weight, came],
        [
            whole(grads),
            pl.BlockSpec((step, width), lambda j, t: (HOP_STEPS * t[0] + j, 0)),
            cols,
        ],
        [jax.ShapeDtypeStruct((rows, width), B16), jax.ShapeDtypeStruct((rows, half), B16)],
        [cols, pl.BlockSpec((rows, half), lambda j, t: (0, 0))],
        [],
        0,
    )


def start_chosen(choice, offers, core, target, done):
    rows, half = target.shape
    for at, offer in enumerate(offers):

        @pl.when(choice == at)
        def _(offer=offer):
            source = offer
            if offer.shape[1] != half:
                source = offer.at[:, pl.ds(pl.multiple_of(core * half, half), half)]
            pltpu.make_async_copy(source, target, done).start()


def wait_chosen(target, done):
    pltpu.make_async_copy(target, target, done).wait()


def piece_body(count, extra, table, *refs):
    ours, theirs = refs[:count], refs[count : 2 * count]
    grads, their_grads = refs[2 * count : 2 * count + 2]
    rest = refs[2 * count + 2 :]
    out, a, b, done = rest[2 * extra], *rest[-3:]
    half = a.shape[1]

    @pl.when(pl.program_id(0) == 0)
    def _():
        start_chosen(table[0], ours, table[1], a, done.at[0])
        start_chosen(table[0], theirs, table[1], b, done.at[1])
        wait_chosen(a, done.at[0])
        wait_chosen(b, done.at[1])

    mix = dot(a[...], grads[...], 0, 0) + dot(b[...], their_grads[...], 0, 0)
    out[...] = mix.astype(B16)
    if extra:
        maps, came, kept, sent = rest[0], rest[1], rest[3], rest[4]
        split = kept.shape[0]
        total = maps[...] + came[...].astype(F32)
        kept[...] = total[:split]
        sent[...] = total[split:].astype(B16)


def piece(table, ours, theirs, grads, their_grads, extra=()):
    rows, width = grads.shape
    half = width // 2

    def cols(count):
        return pl.BlockSpec((count, width // 2), lambda j, t: (0, j))

    split = extra[0].shape[0] // 2 if extra else 0
    outs = [jax.ShapeDtypeStruct((half, width), B16)]
    if extra:
        outs.append(kept_in_hbm(jax.ShapeDtypeStruct((split, width), F32)))
        outs.append(jax.ShapeDtypeStruct((split, width), B16))
    return call(
        functools.partial(piece_body, len(ours), 1 if extra else 0),
        table,
        (2,),
        [*ours, *theirs, grads, their_grads, *extra],
        [pl.BlockSpec(memory_space=pltpu.HBM)] * (2 * len(ours))
        + [cols(rows), cols(rows)]
        + [cols(2 * split)] * len(extra),
        outs,
        [cols(v.shape[0]) for v in outs],
        [pltpu.VMEM((rows, half), B16)] * 2 + [pltpu.SemaphoreType.DMA((2,))],
        0,
        pinned=[*range(2 * len(ours))] + [2 * len(ours) + 2] * (1 if extra else 0),
    )


def query_body(groups, n, half, table, *refs):
    offers, blocks = refs[: -6 - n], refs[-6 - n : -6]
    own_out, other_out, other_end, rows_in, weight_in, done = refs[-6:]
    rows = own_out.shape[0]

    @pl.when(pl.program_id(0) == 0)
    def _():
        at = 0
        waits = []
        for step, count in enumerate(groups):
            start = pl.multiple_of(table[1 + step] * half, half)
            for side in range(2):
                here = offers[at : at + count]
                at += count
                target = rows_in.at[pl.ds(side * rows, rows), pl.ds(start, half)]
                sem = done.at[2 * step + side]
                start_chosen(table[1 + n + step], here, table[0], target, sem)
                waits.append((target, sem))
        for target, sem in waits:
            wait_chosen(target, sem)

    for chunk in range(n):
        weight_in[pl.ds(chunk * half, half), :] = blocks[chunk][...]
    own_out[...] = dot(rows_in[pl.ds(0, rows), :], weight_in[...], 1, 0)
    other = dot(rows_in[pl.ds(rows, rows), :], weight_in[...], 1, 0).astype(B16)
    other_out[...] = other[: rows // 2]
    other_end[...] = other[rows // 2 :]


def query_parts(table, offers, weight):
    n = len(offers)
    rows, width = offers[0][0][0].shape[0], weight.shape[1]
    half = cols = width // 2
    flat = [v for pair in offers for side in pair for v in side]

    def block(chunk):
        return pl.BlockSpec((half, cols), lambda j, t: (2 * chunk + t[0], j))

    out = pl.BlockSpec((rows, cols), lambda j, t: (0, j))
    part = pl.BlockSpec((rows // 2, cols), lambda j, t: (0, j))
    return call(
        functools.partial(query_body, [len(pair[0]) for pair in offers], n, half),
        table,
        (2,),
        [*flat] + [weight] * n,
        [pl.BlockSpec(memory_space=pltpu.HBM)] * len(flat) + [block(c) for c in range(n)],
        [
            kept_in_hbm(jax.ShapeDtypeStruct((rows, width), F32)),
            jax.ShapeDtypeStruct((rows // 2, width), B16),
            jax.ShapeDtypeStruct((rows // 2, width), B16),
        ],
        [out, part, part],
        [
            pltpu.VMEM((2 * rows, n * half), B16),
            pltpu.VMEM((n * half, cols), B16),
            pltpu.SemaphoreType.DMA((2 * n,)),
        ],
        0,
        pinned=range(len(flat)),
        limit=28,
    )


def term_body(table, grads, weight, out):
    out[...] = dot(grads[...], weight[...], 1, 1).astype(B16)


def term_of(table, grads, weight):
    rows, width = grads.shape
    half = width // 2
    return call(
        term_body,
        table,
        (2,),
        [grads, weight],
        [whole(grads), pl.BlockSpec((half, width), lambda j, t: (2 * t[0] + j, 0))],
        kept_in_hbm(jax.ShapeDtypeStruct((rows, width), B16)),
        pl.BlockSpec((rows, half), lambda j, t: (0, j)),
        [],
        2 * rows * width * width,
    )


def into_target(value, target, shape, at, body, extra, outs, steps):
    rows, width = shape[2], shape[1]
    block = rows // steps
    spec = pl.BlockSpec((block, width), lambda i, t: (i, 0))
    arrays, specs, aliases = [value, *extra], [spec] * (1 + len(extra)), {}
    if target is not None:
        aliases = {1 + len(arrays): 0}
        arrays.append(target)
        specs.append(pl.BlockSpec(memory_space=pl.ANY))
    where = pl.BlockSpec((block, width), lambda i, t: (steps * t[0] + i, 0))
    return call(
        body,
        at,
        (steps,),
        arrays,
        specs,
        [jax.ShapeDtypeStruct(shape[:2], B16)] + [jax.ShapeDtypeStruct((rows, width), B16)] * outs,
        [where] + [spec] * outs,
        [],
        0,
        aliases,
    )


def place_body(table, value, *refs):
    refs[-1][...] = value[...]


def place(at, value, target, shape):
    return into_target(value, target, (*shape, value.shape[0]), at, place_body, (), 0, 2)[0]


def sum_body(table, a, b, *refs):
    total = (a[...].astype(F32) + b[...].astype(F32)).astype(B16)
    refs[-2][...] = total
    refs[-1][...] = total


def place_sum(at, a, b, target, shape, rows):
    return into_target(a, target, (*shape, rows), at, sum_body, (b,), 1, 2)


def ranks_body(rank, table, mine, fetched, shared, relative, tokens, grads, down, up, part):
    split = mine.shape[1]
    down[pl.ds(0, split), :] = mine[0]
    up[pl.ds(0, split), :] = mine[1]

    @pl.when(table[0] == 0)
    def _():
        down[pl.ds(split, split), :] = fetched[...]
        up[pl.ds(split, split), :] = shared[...]

    @pl.when(table[0] != 0)
    def _():
        down[pl.ds(split, split), :] = shared[...]
        up[pl.ds(split, split), :] = fetched[...]

    for kind, (maps, rows) in enumerate(((down, tokens), (up, grads))):
        every = dot(maps[...], rows[...], 1, 1)
        total = None
        for slot in range(2 * split // rank):
            own = jnp.where(relative[...] == slot, every[slot * rank : (slot + 1) * rank], 0.0)
            total = own if total is None else total + own
        part[pl.ds(kind * rank, rank), :] = total.astype(B16)


def ranks_of(table, rank, mine, fetched, shared, relative, tokens, grads):
    rows, width = tokens.shape
    arrays = [mine, fetched, shared, relative, tokens, grads]
    outs = [
        jax.ShapeDtypeStruct((2 * mine.shape[1], width), B16),
        jax.ShapeDtypeStruct((2 * mine.shape[1], width), B16),
        jax.ShapeDtypeStruct((2 * rank, rows), B16),
    ]
    body = functools.partial(ranks_body, rank)
    specs = [whole(v) for v in arrays]
    return call(body, table, (1,), arrays, specs, [kept_in_hbm(v) for v in outs], [whole(v) for v in outs], [], 0, pinned=(4,))


def maps_body(rank, count, table, *refs):
    relative, tokens, grads, low, back, kept, sent = refs[count:]
    total = refs[0][...].astype(F32)
    for part in refs[1:count]:
        total += part[...].astype(F32)
    total = total.astype(B16).astype(F32)
    for kind, wide in enumerate((low, back)):
        own = total[kind * rank : (kind + 1) * rank]
        for slot in range(wide.shape[0] // rank):
            spread_out = jnp.where(relative[...] == slot, own, 0.0)
            wide[pl.ds(slot * rank, rank), :] = spread_out.astype(B16)
    for kind, (wide, rows) in enumerate(((back, tokens), (low, grads))):
        term = SCALE * dot(wide[...], rows[...], 1, 0)

        @pl.when(table[0] == kind)
        def _(term=term):
            kept[...] = term

        @pl.when(table[0] != kind)
        def _(term=term):
            sent[...] = term.astype(B16)


def maps_of(table, rank, slots, parts, relative, tokens, grads):
    rows, width = tokens.shape
    arrays = [*parts, relative, tokens, grads]
    outs = [
        jax.ShapeDtypeStruct((slots * rank, rows), B16),
        jax.ShapeDtypeStruct((slots * rank, rows), B16),
        jax.ShapeDtypeStruct((slots * rank, width), F32),
        jax.ShapeDtypeStruct((slots * rank, width), B16),
    ]
    body = functools.partial(maps_body, rank, len(parts))
    specs = [whole(v) for v in arrays]
    return call(body, table, (1,), arrays, specs, [kept_in_hbm(v) for v in outs], [whole(v) for v in outs], [], 0, pinned=(len(parts) + 1,))


def lora_body(table, low, up, back, down, out, into):
    out[...] = (SCALE * dot(low[...], up[...], 0, 0)).astype(B16)
    into[...] = (SCALE * dot(back[...], down[...], 0, 0)).astype(B16)


def lora_of(low, up, back, down):
    rows, width = low.shape[1], up.shape[1]
    arrays = [low, up, back, down]
    out = jax.ShapeDtypeStruct((rows, width), B16)
    specs = [whole(v) for v in arrays]
    table = jnp.zeros((1,), jnp.int32)
    return call(lora_body, table, (1,), arrays, specs, [kept_in_hbm(out)] * 2, [whole(out)] * 2, [], 0)


def finish_body(table, here, live, out_lora, term, in_lora, ends, there, there_end, theirs, theirs_end, kept, other, query, token_grad, down, up):
    for i, (mine, sums) in enumerate(((there, theirs), (there_end, theirs_end))):

        @pl.when(pl.program_id(0) == i)
        def _(mine=mine, sums=sums):
            total = here[...] + mine[...].astype(F32) + out_lora[...].astype(F32)
            query[...] = jnp.where(live[...] > 0, total, 0.0).astype(B16)
            total = term[...].astype(F32) + in_lora[...].astype(F32) + ends[...].astype(F32)
            token_grad[...] = (total + sums[...].astype(F32)).astype(B16)

    @pl.when((pl.program_id(0) == 0) & (table[0] == 0))
    def _():
        down[...] = kept[...]
        up[...] = other[...]

    @pl.when((pl.program_id(0) == 0) & (table[0] != 0))
    def _():
        down[...] = other[...]
        up[...] = kept[...]


def finish(core, here, live, out_lora, term, in_lora, ends, *rest):
    rows, width = here.shape
    kept = rest[-1]
    spec = pl.BlockSpec((rows // 2, width), lambda i, t: (i, 0))
    thin = pl.BlockSpec((rows // 2, 1), lambda i, t: (i, 0))
    out = jax.ShapeDtypeStruct((rows, width), B16)
    small = jax.ShapeDtypeStruct(kept.shape, F32)
    return call(
        finish_body,
        core[None],
        (2,),
        [here, live, out_lora, term, in_lora, ends, *rest],
        [spec, thin, spec, spec, spec, spec] + [whole(v) for v in rest],
        [out, out, small, small],
        [spec, spec, whole(small), whole(small)],
        [],
        0,
    )


def add_body(table, a, b, out):
    out[...] = (a[...].astype(F32) + b[...].astype(F32)).astype(B16)


def add(a, b):
    rows, width = a.shape
    spec = pl.BlockSpec((rows // 2, width), lambda i, t: (i, 0))
    out = jax.ShapeDtypeStruct(a.shape, B16)
    table = jnp.zeros((1,), jnp.int32)
    return call(add_body, table, (2,), [a, b], [spec] * 2, out, spec, [], 0, pinned=(0, 1))


def mask_body(tenants, slots, table, mine, theirs, grads, their_grads, slot_rows, live):
    blocks = mine.shape[0] // BLOCK_ROWS
    row = lax.broadcasted_iota(jnp.int32, (BLOCK_ROWS, 1), 0)
    for side, (rows_in, rows_out) in enumerate(((mine, grads), (theirs, their_grads))):
        for b in range(blocks):
            block = table[2 * tenants + side] + b
            start = jnp.int32(0)
            left = slot = jnp.int32(0)
            for t in range(tenants):
                here = start <= block
                left = jnp.where(here, table[t] - BLOCK_ROWS * (block - start), left)
                slot = jnp.where(here, table[tenants + t], slot)
                start = start + (table[t] + BLOCK_ROWS - 1) // BLOCK_ROWS
            at = pl.ds(b * BLOCK_ROWS, BLOCK_ROWS)
            alive = row < left
            rows_out[at, :] = jnp.where(alive, rows_in[at, :].astype(F32), 0.0).astype(B16)
            if side == 0:
                live[at, :] = jnp.where(alive, 1.0, 0.0)
                placed = lax.rem(slot + table[2 * tenants + 2], slots)
                slot_rows[:, at] = jnp.full((1, BLOCK_ROWS), placed, jnp.int32)


def masked(table, tenants, slots, mine, theirs):
    rows, width = mine.shape
    outs = [
        jax.ShapeDtypeStruct((rows, width), B16),
        jax.ShapeDtypeStruct((rows, width), B16),
        jax.ShapeDtypeStruct((1, rows), jnp.int32),
        jax.ShapeDtypeStruct((rows, 1), F32),
    ]
    body = functools.partial(mask_body, tenants, slots)
    specs = [whole(mine), whole(theirs)]
    return call(body, table, (1,), [mine, theirs], specs, [*outs[:3], kept_in_hbm(outs[3])], [whole(v) for v in outs], [], 0, pinned=(0, 1))


def kept_in_hbm(shape):
    return pltpu.HBM(shape.shape, shape.dtype)


def shards_line(tokens, weight, down_maps, up_maps, counts, slot_of, cotangent):
    rows, width = tokens.shape
    held, _, rank = down_maps.shape
    n = lax.axis_size("tensor")
    slots = held * 2
    z = lax.axis_index("tensor")
    owner = lax.axis_index("tenant")
    core = lax.axis_index("dp")
    swap = [(0, 1), (1, 0)]
    ahead = jnp.where(core == 0, z, n - 1 - z)
    line_pairs = []
    for i in range(n - 1):
        line_pairs += [(2 * i, 2 * i + 2), (2 * i + 3, 2 * i + 1)]

    def along(value):
        return lax.ppermute(value, ("tensor", "dp"), line_pairs)

    def other_tenant(value):
        return lax.ppermute(value, "tenant", swap)

    def other_core(value):
        return lax.ppermute(value, "dp", swap)

    def numbers(*values):
        return jnp.stack([v.astype(jnp.int32) for v in values])

    chunk_of = [z]
    choice_of = [jnp.zeros((), jnp.int32)]
    kinds_of = [None]
    for choices in arrival_plan(n):
        kinds = sorted({(t, d == c) for t, d, _ in choices for c in range(2)})
        chunk = choice = jnp.zeros((), jnp.int32)
        for at, (t, direction, source) in enumerate(choices):
            chunk = jnp.where(z == at, source, chunk)
            for c in range(2):
                here = (z == at) & (core == c)
                choice = jnp.where(here, kinds.index((t, direction == c)), choice)
        chunk_of.append(chunk)
        choice_of.append(choice)
        kinds_of.append(kinds)

    st = {}

    def fence():
        names = [name for name in st if name not in FREE]
        st.update(zip(names, lax.optimization_barrier([st[name] for name in names])))

    def hop_of(k):
        t, side = k // 2 + 1, k % 2
        chunk = jnp.clip(n + ahead + 1 - t, 0, n - 1)
        chunk = jnp.where(core == 0, chunk, n - 1 - chunk)
        sums = (ahead < n - 1) & (ahead < t - 1)
        table = numbers(chunk, sums, 1 - core)
        grads = st["their_grads" if side else "grads"]
        st["sent"], st["share"] = hop(table, grads, st["weight"], st["line", t - 1, side])

    def offers_of(step):
        if step == 0:
            return [[st["tokens"]], [st["their_tokens"]]]
        kinds = kinds_of[step]
        return [
            [st["line", t, s] if mine else st["shared", t, 1 - s] for t, mine in kinds]
            for s in range(2)
        ]

    def piece_of(step, extra=()):
        table = numbers(choice_of[step], core)
        both = st["grads"], st["their_grads"]
        st["mix", step], *st["kept"] = piece(table, *offers_of(step), *both, extra)

    def sum_of(step):
        at = (2 * chunk_of[step] + core)[None]
        pair = st.pop(("mix", step)), st.pop(("x", step))
        shape = n * width, width
        st["wg"], st["ours", step] = place_sum(at, *pair, st.get("wg"), shape, width // 2)

    def place_of(step, theirs):
        at = (2 * chunk_of[step] + 1 - core)[None]
        st["wg"] = place(at, theirs, st["wg"], (n * width, width))

    st["weight"], st["tokens"], st["z"] = weight, tokens, z
    line = along(tokens)
    st["their_tokens"] = other_core(tokens)
    theirs = other_core(cotangent)
    mine = jnp.stack([jnp.swapaxes(down_maps, 1, 2), up_maps]).reshape(2, -1, width)
    st["fetched"] = other_tenant(lax.dynamic_index_in_dim(mine, core, 0, keepdims=False))
    st["mine"] = mine
    blocks = rows // BLOCK_ROWS
    first = (owner * 2 + core) * blocks
    their_first = (owner * 2 + 1 - core) * blocks
    places = numbers(first, their_first, (2 - owner) * held)
    table = jnp.concatenate([counts, slot_of, places])
    st["grads"], st["their_grads"], st["relative"], st["live"] = masked(
        table, counts.shape[0], slots, cotangent, theirs
    )
    fence()

    coming = along(st["their_tokens"])
    piece_of(0)
    swapped = other_tenant(st["mix", 0])
    shared = other_core(st["fetched"])
    names = ("relative", "tokens", "grads")
    st["down"], st["up"], st["part"] = ranks_of(
        core[None], rank, st.pop("mine"), st.pop("fetched"), shared, *[st[v] for v in names]
    )
    st["line", 1, 0] = line
    line = coming
    fence()

    wg_share = None
    for k in range(2, 2 * n + 1):
        t, side, step = k // 2 + 1, k % 2, k // 2
        last = k == 2 * n
        if not last:
            hop_of(k)
        if k == 2:
            for d in range(1, n):
                pairs = [(i, (i + d) % n) for i in range(n)]
                st["part", d] = lax.ppermute(st["part"], "tensor", pairs)
        if k == 3:
            st["x", 0] = swapped
        if k == 6:
            st["maps_x"] = other_tenant(st["kept"].pop())
        fence()
        if k == 6:
            swapped = other_tenant(st["mix", 2])
        if not last:
            coming = along(st.pop("sent"))
            st["shared", t - 1, side] = other_core(st.pop("share"))
        if side == 1:
            extra = ()
            if step == 2:
                extra = st.pop("maps"), st.pop("came")
            if step == n - 1:
                kept = st.pop("kept")
            piece_of(step, extra)
            if step == n - 1:
                st["kept"] = kept[:1]
            if step > 1:
                st["x", step - 1] = swapped
            fence()
            if step != 2:
                swapped = other_tenant(st["mix", step])
            sum_of(step - 1)
        elif 4 <= k < 2 * n:
            wg_share = other_core(st["ours", step - 2])
        if k >= 6 and side == 0:
            place_of(step - 3, st.pop("theirs"))
        if k == 2:
            st["low"], st["back"], st["maps"], st["for_sibling"] = maps_of(
                core[None],
                rank,
                slots,
                [st.pop("part")] + [st.pop(("part", d)) for d in range(1, n)],
                *[st[v] for v in names],
            )
            st["came"] = other_core(st.pop("for_sibling"))
        if k == 4:
            st["term"] = term_of(st["z"][None], st["grads"], st["weight"])
        if k == 6:
            maps = [st.pop(v) for v in ("low", "up", "back", "down")]
            st["lora_out"], st["lora_in"] = lora_of(*maps)
        if last:
            offers = [offers_of(s) for s in range(n)]
            table = numbers(core, *chunk_of, *choice_of)
            st["query_here"], *st["query_there"] = query_parts(table, offers, st["weight"])
        st["line", (k - 1) // 2 + 1, 1 - side] = line
        line = coming
        if side == 1 and wg_share is not None:
            st["theirs"] = wg_share
            wg_share = None
        fence()

    kept = st.pop("kept")[0] + st.pop("maps_x").astype(F32)
    other = other_core(kept)
    there = [other_core(v) for v in st.pop("query_there")]
    theirs = [other_core(v) for v in jnp.split(st["line", n, 1], 2)]
    sums = [st.pop(v) for v in ("query_here", "live", "lora_out", "term", "lora_in")]
    ends = st["line", n, 0]
    done = finish(core, *sums, ends, *there, *theirs, kept, other)
    st["query"], st["token_grad"], down_grad, up_grad = done
    st["down_grad"] = jnp.swapaxes(down_grad.reshape(held, rank, width), 1, 2)
    st["up_grad"] = up_grad.reshape(held, rank, width)
    fence()
    st["x", n - 1] = swapped
    fence()
    st["ours", n - 1] = add(st["mix", n - 1], st["x", n - 1])
    earlier = other_core(st["ours", n - 2])
    theirs = other_core(st["ours", n - 1])
    shape = n * width, width
    mine_at = (2 * chunk_of[n - 1] + core)[None]
    st["wg"] = place(mine_at, st["ours", n - 1], st["wg"], shape)
    place_of(n - 2, earlier)
    place_of(n - 1, theirs)
    return st["query"], st["token_grad"], st["wg"], st["down_grad"], st["up_grad"]


def solution(mesh):
    placed = (
        P(("groups", "tenant", "dp"), "tensor"),
        P(None, "tensor"),
        P("tenant", "tensor", None),
        P("tenant", None, "tensor"),
        P("groups"),
        P(),
        P(("groups", "tenant", "dp"), "tensor"),
    )
    short = mesh.shape["tensor"] == 4
    paired = mesh.shape["tenant"] == 2 and mesh.shape["dp"] == 2
    return jax.shard_map(
        shards_line if short and paired else shards_general,
        mesh=mesh,
        in_specs=placed,
        out_specs=(
            P(("groups", "tenant", "dp"), "tensor"),
            P(("groups", "tenant", "dp"), "tensor"),
            P("groups", "tensor"),
            P(("groups", "tenant"), "tensor", None),
            P(("groups", "tenant"), None, "tensor"),
        ),
        check_vma=False,
    )
```

```python
import functools

import jax
import jax.numpy as jnp
from jax import lax
from jax.experimental import pallas as pl
from jax.experimental.pallas import tpu as pltpu
from jax.sharding import PartitionSpec as P

BLOCK_ROWS = 128
SCALE = 2.0
F32 = jnp.float32
B16 = jnp.bfloat16


def dot(a, b, ca, cb):
    return lax.dot_general(a, b, (((ca,), (cb,)), ((), ())), preferred_element_type=F32)


def lookup(source, position):
    match_mask = position[..., None] == jnp.arange(source.shape[0], dtype=jnp.int32)
    return jnp.sum(jnp.where(match_mask, source, 0), axis=-1)


def layout(tenant_row_counts, row_ids):
    block_count = (tenant_row_counts + BLOCK_ROWS - 1) // BLOCK_ROWS
    segment_offset = jnp.cumsum(block_count) - block_count
    block_ids = row_ids // BLOCK_ROWS
    tenant_of = (
        jnp.sum((segment_offset[None, :] <= block_ids[:, None]).astype(jnp.int32), axis=1) - 1
    )
    offset = row_ids - BLOCK_ROWS * lookup(segment_offset, tenant_of)
    return tenant_of, offset < lookup(tenant_row_counts, tenant_of)


def rank_partials(maps, rows, mask, slots):
    every = dot(maps, rows, 1, 1)
    every = every.reshape(slots, -1, rows.shape[0])
    return jnp.sum(jnp.where(mask[:, None, :], every, 0.0), axis=0)


def spread(values, mask):
    wide = jnp.where(mask[:, None, :], values[None], jnp.zeros((), values.dtype))
    return wide.reshape(-1, values.shape[-1])


def shards_general(tokens, weight, down_maps, up_maps, counts, slot_of, cotangent):
    rows, width = tokens.shape
    held, _, rank = down_maps.shape
    slots = held * lax.axis_size("tenant")
    owner = lax.axis_index("tenant")
    row_ids = lax.axis_index(("tenant", "dp")) * rows + jnp.arange(rows, dtype=jnp.int32)
    tenant, live = layout(counts, row_ids)
    slot = lookup(slot_of, tenant)
    mask = slot[None, :] == jnp.arange(slots, dtype=jnp.int32)[:, None]
    grads = jnp.where(live[:, None], cotangent, jnp.zeros_like(cotangent))
    kept = jnp.where(live[:, None], tokens, jnp.zeros_like(tokens))
    down = lax.all_gather(jnp.swapaxes(down_maps, 1, 2), "tenant", axis=0, tiled=True)
    up = lax.all_gather(up_maps, "tenant", axis=0, tiled=True)
    down, up = down.reshape(-1, width), up.reshape(-1, width)
    gathered = lax.all_gather(kept, "tensor", axis=1, tiled=True)
    part = jnp.stack(
        [rank_partials(down, kept, mask, slots), rank_partials(up, grads, mask, slots)]
    )
    low, back = lax.psum(part.astype(B16), "tensor")
    low, back = spread(low, mask), spread(back, mask)
    base = dot(gathered, weight, 1, 0)
    query = (base + (SCALE * dot(low, up, 0, 0)).astype(B16).astype(F32)).astype(B16)
    term = dot(grads, weight, 1, 1).astype(B16)
    summed = lax.psum_scatter(term, "tensor", scatter_dimension=1, tiled=True).astype(F32)
    lora = (SCALE * dot(back, down, 0, 0)).astype(B16).astype(F32)
    token_grad = jnp.where(live[:, None], summed + lora, 0.0).astype(B16)
    axes = ("tenant", "dp")
    weight_grad = lax.psum(dot(gathered, grads, 0, 0).astype(B16), axes)
    maps = jnp.stack([SCALE * dot(back, kept, 1, 0), SCALE * dot(low, grads, 1, 0)])
    maps = lax.psum(maps.astype(B16), axes).astype(F32).reshape(2, slots, rank, width)
    maps = lax.dynamic_slice_in_dim(maps, owner * held, held, 1)
    return query, token_grad, weight_grad, jnp.swapaxes(maps[0], 1, 2), maps[1]


def arrival_plan(n):
    plan = [[] for _ in range(n - 1)]
    for z in range(n):
        seen = []
        for t in range(1, n):
            if z - t >= 0:
                seen.append((t, 0, z - t))
            if z + t < n:
                seen.append((t, 1, z + t))
        for step, entry in enumerate(seen):
            plan[step].append(entry)
    return plan


def whole(array):
    return pl.BlockSpec(array.shape, lambda *_: (0,) * array.ndim)


def call(body, table, grid, arrays, specs, outs, out_specs, scratch, flops, aliases=None, pinned=(), limit=48):
    arrays = list(arrays)
    for at in pinned:
        arrays[at] = pltpu.with_memory_space_constraint(arrays[at], pltpu.HBM)
    return pl.pallas_call(
        body,
        grid_spec=pltpu.PrefetchScalarGridSpec(
            num_scalar_prefetch=1,
            grid=grid,
            in_specs=specs,
            out_specs=out_specs,
            scratch_shapes=scratch,
        ),
        out_shape=outs,
        input_output_aliases=aliases or {},
        compiler_params=pltpu.CompilerParams(vmem_limit_bytes=limit * 1024 * 1024),
        cost_estimate=pl.CostEstimate(flops=1, bytes_accessed=1, transcendentals=0),
    )(table, *arrays)


FREE = ()
HOP_STEPS = 2


def hop_body(table, grads, weight, came, goes, share):
    @pl.when(pl.program_id(0) == table[2])
    def _():
        share[...] = came[...]

    @pl.when(table[1] == 0)
    def _():
        goes[...] = came[...]

    @pl.when(table[1] != 0)
    def _():
        term = dot(grads[...], weight[...], 1, 1)
        goes[...] = (term + came[...].astype(F32)).astype(B16)


def hop(table, grads, weight, came):
    rows, width = came.shape
    half, step = width // 2, width // HOP_STEPS
    cols = pl.BlockSpec((rows, step), lambda j, t: (0, j))
    return call(
        hop_body,
        table,
        (HOP_STEPS,),
        [grads, weight, came],
        [
            whole(grads),
            pl.BlockSpec((step, width), lambda j, t: (HOP_STEPS * t[0] + j, 0)),
            cols,
        ],
        [jax.ShapeDtypeStruct((rows, width), B16), jax.ShapeDtypeStruct((rows, half), B16)],
        [cols, pl.BlockSpec((rows, half), lambda j, t: (0, 0))],
        [],
        0,
    )


def start_chosen(choice, offers, core, target, done):
    rows, half = target.shape
    for at, offer in enumerate(offers):

        @pl.when(choice == at)
        def _(offer=offer):
            source = offer
            if offer.shape[1] != half:
                source = offer.at[:, pl.ds(pl.multiple_of(core * half, half), half)]
            pltpu.make_async_copy(source, target, done).start()


def wait_chosen(target, done):
    pltpu.make_async_copy(target, target, done).wait()


def piece_body(count, extra, table, *refs):
    ours, theirs = refs[:count], refs[count : 2 * count]
    grads, their_grads = refs[2 * count : 2 * count + 2]
    rest = refs[2 * count + 2 :]
    out, a, b, done = rest[2 * extra], *rest[-3:]
    half = a.shape[1]

    @pl.when(pl.program_id(0) == 0)
    def _():
        start_chosen(table[0], ours, table[1], a, done.at[0])
        start_chosen(table[0], theirs, table[1], b, done.at[1])
        wait_chosen(a, done.at[0])
        wait_chosen(b, done.at[1])

    mix = dot(a[...], grads[...], 0, 0) + dot(b[...], their_grads[...], 0, 0)
    out[...] = mix.astype(B16)
    if extra:
        maps, came, kept, sent = rest[0], rest[1], rest[3], rest[4]
        split = kept.shape[0]
        total = maps[...] + came[...].astype(F32)
        kept[...] = total[:split]
        sent[...] = total[split:].astype(B16)


def piece(table, ours, theirs, grads, their_grads, extra=()):
    rows, width = grads.shape
    half = width // 2

    def cols(count):
        return pl.BlockSpec((count, width // 2), lambda j, t: (0, j))

    split = extra[0].shape[0] // 2 if extra else 0
    outs = [jax.ShapeDtypeStruct((half, width), B16)]
    if extra:
        outs.append(kept_in_hbm(jax.ShapeDtypeStruct((split, width), F32)))
        outs.append(jax.ShapeDtypeStruct((split, width), B16))
    return call(
        functools.partial(piece_body, len(ours), 1 if extra else 0),
        table,
        (2,),
        [*ours, *theirs, grads, their_grads, *extra],
        [pl.BlockSpec(memory_space=pltpu.HBM)] * (2 * len(ours))
        + [cols(rows), cols(rows)]
        + [cols(2 * split)] * len(extra),
        outs,
        [cols(v.shape[0]) for v in outs],
        [pltpu.VMEM((rows, half), B16)] * 2 + [pltpu.SemaphoreType.DMA((2,))],
        0,
        pinned=[*range(2 * len(ours))] + [2 * len(ours) + 2] * (1 if extra else 0),
    )


def query_body(groups, n, half, table, *refs):
    offers, blocks = refs[: -6 - n], refs[-6 - n : -6]
    own_out, other_out, other_end, rows_in, weight_in, done = refs[-6:]
    rows = own_out.shape[0]

    @pl.when(pl.program_id(0) == 0)
    def _():
        at = 0
        waits = []
        for step, count in enumerate(groups):
            start = pl.multiple_of(table[1 + step] * half, half)
            for side in range(2):
                here = offers[at : at + count]
                at += count
                target = rows_in.at[pl.ds(side * rows, rows), pl.ds(start, half)]
                sem = done.at[2 * step + side]
                start_chosen(table[1 + n + step], here, table[0], target, sem)
                waits.append((target, sem))
        for target, sem in waits:
            wait_chosen(target, sem)

    for chunk in range(n):
        weight_in[pl.ds(chunk * half, half), :] = blocks[chunk][...]
    own_out[...] = dot(rows_in[pl.ds(0, rows), :], weight_in[...], 1, 0)
    other = dot(rows_in[pl.ds(rows, rows), :], weight_in[...], 1, 0).astype(B16)
    other_out[...] = other[: rows // 2]
    other_end[...] = other[rows // 2 :]


def query_parts(table, offers, weight):
    n = len(offers)
    rows, width = offers[0][0][0].shape[0], weight.shape[1]
    half = cols = width // 2
    flat = [v for pair in offers for side in pair for v in side]

    def block(chunk):
        return pl.BlockSpec((half, cols), lambda j, t: (2 * chunk + t[0], j))

    out = pl.BlockSpec((rows, cols), lambda j, t: (0, j))
    part = pl.BlockSpec((rows // 2, cols), lambda j, t: (0, j))
    return call(
        functools.partial(query_body, [len(pair[0]) for pair in offers], n, half),
        table,
        (2,),
        [*flat] + [weight] * n,
        [pl.BlockSpec(memory_space=pltpu.HBM)] * len(flat) + [block(c) for c in range(n)],
        [
            kept_in_hbm(jax.ShapeDtypeStruct((rows, width), F32)),
            jax.ShapeDtypeStruct((rows // 2, width), B16),
            jax.ShapeDtypeStruct((rows // 2, width), B16),
        ],
        [out, part, part],
        [
            pltpu.VMEM((2 * rows, n * half), B16),
            pltpu.VMEM((n * half, cols), B16),
            pltpu.SemaphoreType.DMA((2 * n,)),
        ],
        0,
        pinned=range(len(flat)),
        limit=28,
    )


def term_body(table, grads, weight, out):
    out[...] = dot(grads[...], weight[...], 1, 1).astype(B16)


def term_of(table, grads, weight):
    rows, width = grads.shape
    half = width // 2
    return call(
        term_body,
        table,
        (2,),
        [grads, weight],
        [whole(grads), pl.BlockSpec((half, width), lambda j, t: (2 * t[0] + j, 0))],
        kept_in_hbm(jax.ShapeDtypeStruct((rows, width), B16)),
        pl.BlockSpec((rows, half), lambda j, t: (0, j)),
        [],
        2 * rows * width * width,
    )


def into_target(value, target, shape, at, body, extra, outs, steps):
    rows, width = shape[2], shape[1]
    block = rows // steps
    spec = pl.BlockSpec((block, width), lambda i, t: (i, 0))
    arrays, specs, aliases = [value, *extra], [spec] * (1 + len(extra)), {}
    if target is not None:
        aliases = {1 + len(arrays): 0}
        arrays.append(target)
        specs.append(pl.BlockSpec(memory_space=pl.ANY))
    where = pl.BlockSpec((block, width), lambda i, t: (steps * t[0] + i, 0))
    return call(
        body,
        at,
        (steps,),
        arrays,
        specs,
        [jax.ShapeDtypeStruct(shape[:2], B16)] + [jax.ShapeDtypeStruct((rows, width), B16)] * outs,
        [where] + [spec] * outs,
        [],
        0,
        aliases,
    )


def place_body(table, value, *refs):
    refs[-1][...] = value[...]


def place(at, value, target, shape):
    return into_target(value, target, (*shape, value.shape[0]), at, place_body, (), 0, 2)[0]


def sum_body(table, a, b, *refs):
    total = (a[...].astype(F32) + b[...].astype(F32)).astype(B16)
    refs[-2][...] = total
    refs[-1][...] = total


def place_sum(at, a, b, target, shape, rows):
    return into_target(a, target, (*shape, rows), at, sum_body, (b,), 1, 2)


def ranks_body(rank, table, mine, fetched, shared, relative, tokens, grads, down, up, part):
    split = mine.shape[1]
    down[pl.ds(0, split), :] = mine[0]
    up[pl.ds(0, split), :] = mine[1]

    @pl.when(table[0] == 0)
    def _():
        down[pl.ds(split, split), :] = fetched[...]
        up[pl.ds(split, split), :] = shared[...]

    @pl.when(table[0] != 0)
    def _():
        down[pl.ds(split, split), :] = shared[...]
        up[pl.ds(split, split), :] = fetched[...]

    for kind, (maps, rows) in enumerate(((down, tokens), (up, grads))):
        every = dot(maps[...], rows[...], 1, 1)
        total = None
        for slot in range(2 * split // rank):
            own = jnp.where(relative[...] == slot, every[slot * rank : (slot + 1) * rank], 0.0)
            total = own if total is None else total + own
        part[pl.ds(kind * rank, rank), :] = total.astype(B16)


def ranks_of(table, rank, mine, fetched, shared, relative, tokens, grads):
    rows, width = tokens.shape
    arrays = [mine, fetched, shared, relative, tokens, grads]
    outs = [
        jax.ShapeDtypeStruct((2 * mine.shape[1], width), B16),
        jax.ShapeDtypeStruct((2 * mine.shape[1], width), B16),
        jax.ShapeDtypeStruct((2 * rank, rows), B16),
    ]
    body = functools.partial(ranks_body, rank)
    specs = [whole(v) for v in arrays]
    return call(body, table, (1,), arrays, specs, [kept_in_hbm(v) for v in outs], [whole(v) for v in outs], [], 0, pinned=(4,))


def maps_body(rank, count, table, *refs):
    relative, tokens, grads, low, back, kept, sent = refs[count:]
    total = refs[0][...].astype(F32)
    for part in refs[1:count]:
        total += part[...].astype(F32)
    total = total.astype(B16).astype(F32)
    for kind, wide in enumerate((low, back)):
        own = total[kind * rank : (kind + 1) * rank]
        for slot in range(wide.shape[0] // rank):
            spread_out = jnp.where(relative[...] == slot, own, 0.0)
            wide[pl.ds(slot * rank, rank), :] = spread_out.astype(B16)
    for kind, (wide, rows) in enumerate(((back, tokens), (low, grads))):
        term = SCALE * dot(wide[...], rows[...], 1, 0)

        @pl.when(table[0] == kind)
        def _(term=term):
            kept[...] = term

        @pl.when(table[0] != kind)
        def _(term=term):
            sent[...] = term.astype(B16)


def maps_of(table, rank, slots, parts, relative, tokens, grads):
    rows, width = tokens.shape
    arrays = [*parts, relative, tokens, grads]
    outs = [
        jax.ShapeDtypeStruct((slots * rank, rows), B16),
        jax.ShapeDtypeStruct((slots * rank, rows), B16),
        jax.ShapeDtypeStruct((slots * rank, width), F32),
        jax.ShapeDtypeStruct((slots * rank, width), B16),
    ]
    body = functools.partial(maps_body, rank, len(parts))
    specs = [whole(v) for v in arrays]
    return call(body, table, (1,), arrays, specs, [kept_in_hbm(v) for v in outs], [whole(v) for v in outs], [], 0, pinned=(len(parts) + 1,))


def lora_body(table, low, up, back, down, out, into):
    out[...] = (SCALE * dot(low[...], up[...], 0, 0)).astype(B16)
    into[...] = (SCALE * dot(back[...], down[...], 0, 0)).astype(B16)


def lora_of(low, up, back, down):
    rows, width = low.shape[1], up.shape[1]
    arrays = [low, up, back, down]
    out = jax.ShapeDtypeStruct((rows, width), B16)
    specs = [whole(v) for v in arrays]
    table = jnp.zeros((1,), jnp.int32)
    return call(lora_body, table, (1,), arrays, specs, [kept_in_hbm(out)] * 2, [whole(out)] * 2, [], 0)


def finish_body(table, here, live, out_lora, term, in_lora, ends, there, there_end, theirs, theirs_end, kept, other, query, token_grad, down, up):
    for i, (mine, sums) in enumerate(((there, theirs), (there_end, theirs_end))):

        @pl.when(pl.program_id(0) == i)
        def _(mine=mine, sums=sums):
            total = here[...] + mine[...].astype(F32) + out_lora[...].astype(F32)
            query[...] = jnp.where(live[...] > 0, total, 0.0).astype(B16)
            total = term[...].astype(F32) + in_lora[...].astype(F32) + ends[...].astype(F32)
            token_grad[...] = (total + sums[...].astype(F32)).astype(B16)

    @pl.when((pl.program_id(0) == 0) & (table[0] == 0))
    def _():
        down[...] = kept[...]
        up[...] = other[...]

    @pl.when((pl.program_id(0) == 0) & (table[0] != 0))
    def _():
        down[...] = other[...]
        up[...] = kept[...]


def finish(core, here, live, out_lora, term, in_lora, ends, *rest):
    rows, width = here.shape
    kept = rest[-1]
    spec = pl.BlockSpec((rows // 2, width), lambda i, t: (i, 0))
    thin = pl.BlockSpec((rows // 2, 1), lambda i, t: (i, 0))
    out = jax.ShapeDtypeStruct((rows, width), B16)
    small = jax.ShapeDtypeStruct(kept.shape, F32)
    return call(
        finish_body,
        core[None],
        (2,),
        [here, live, out_lora, term, in_lora, ends, *rest],
        [spec, thin, spec, spec, spec, spec] + [whole(v) for v in rest],
        [out, out, small, small],
        [spec, spec, whole(small), whole(small)],
        [],
        0,
    )


def add_body(table, a, b, out):
    out[...] = (a[...].astype(F32) + b[...].astype(F32)).astype(B16)


def add(a, b):
    rows, width = a.shape
    spec = pl.BlockSpec((rows // 2, width), lambda i, t: (i, 0))
    out = jax.ShapeDtypeStruct(a.shape, B16)
    table = jnp.zeros((1,), jnp.int32)
    return call(add_body, table, (2,), [a, b], [spec] * 2, out, spec, [], 0, pinned=(0, 1))


def mask_body(tenants, slots, table, mine, theirs, grads, their_grads, slot_rows, live):
    blocks = mine.shape[0] // BLOCK_ROWS
    row = lax.broadcasted_iota(jnp.int32, (BLOCK_ROWS, 1), 0)
    for side, (rows_in, rows_out) in enumerate(((mine, grads), (theirs, their_grads))):
        for b in range(blocks):
            block = table[2 * tenants + side] + b
            start = jnp.int32(0)
            left = slot = jnp.int32(0)
            for t in range(tenants):
                here = start <= block
                left = jnp.where(here, table[t] - BLOCK_ROWS * (block - start), left)
                slot = jnp.where(here, table[tenants + t], slot)
                start = start + (table[t] + BLOCK_ROWS - 1) // BLOCK_ROWS
            at = pl.ds(b * BLOCK_ROWS, BLOCK_ROWS)
            alive = row < left
            rows_out[at, :] = jnp.where(alive, rows_in[at, :].astype(F32), 0.0).astype(B16)
            if side == 0:
                live[at, :] = jnp.where(alive, 1.0, 0.0)
                placed = lax.rem(slot + table[2 * tenants + 2], slots)
                slot_rows[:, at] = jnp.full((1, BLOCK_ROWS), placed, jnp.int32)


def masked(table, tenants, slots, mine, theirs):
    rows, width = mine.shape
    outs = [
        jax.ShapeDtypeStruct((rows, width), B16),
        jax.ShapeDtypeStruct((rows, width), B16),
        jax.ShapeDtypeStruct((1, rows), jnp.int32),
        jax.ShapeDtypeStruct((rows, 1), F32),
    ]
    body = functools.partial(mask_body, tenants, slots)
    specs = [whole(mine), whole(theirs)]
    return call(body, table, (1,), [mine, theirs], specs, [*outs[:3], kept_in_hbm(outs[3])], [whole(v) for v in outs], [], 0, pinned=(0, 1))


def kept_in_hbm(shape):
    return pltpu.HBM(shape.shape, shape.dtype)


def shards_line(tokens, weight, down_maps, up_maps, counts, slot_of, cotangent):
    rows, width = tokens.shape
    held, _, rank = down_maps.shape
    n = lax.axis_size("tensor")
    slots = held * 2
    z = lax.axis_index("tensor")
    owner = lax.axis_index("tenant")
    core = lax.axis_index("dp")
    swap = [(0, 1), (1, 0)]
    ahead = jnp.where(core == 0, z, n - 1 - z)
    line_pairs = []
    for i in range(n - 1):
        line_pairs += [(2 * i, 2 * i + 2), (2 * i + 3, 2 * i + 1)]

    def along(value):
        return lax.ppermute(value, ("tensor", "dp"), line_pairs)

    def other_tenant(value):
        return lax.ppermute(value, "tenant", swap)

    def other_core(value):
        return lax.ppermute(value, "dp", swap)

    def numbers(*values):
        return jnp.stack([v.astype(jnp.int32) for v in values])

    chunk_of = [z]
    choice_of = [jnp.zeros((), jnp.int32)]
    kinds_of = [None]
    for choices in arrival_plan(n):
        kinds = sorted({(t, d == c) for t, d, _ in choices for c in range(2)})
        chunk = choice = jnp.zeros((), jnp.int32)
        for at, (t, direction, source) in enumerate(choices):
            chunk = jnp.where(z == at, source, chunk)
            for c in range(2):
                here = (z == at) & (core == c)
                choice = jnp.where(here, kinds.index((t, direction == c)), choice)
        chunk_of.append(chunk)
        choice_of.append(choice)
        kinds_of.append(kinds)

    st = {}

    def fence():
        names = [name for name in st if name not in FREE]
        st.update(zip(names, lax.optimization_barrier([st[name] for name in names])))

    def hop_of(k):
        t, side = k // 2 + 1, k % 2
        chunk = jnp.clip(n + ahead + 1 - t, 0, n - 1)
        chunk = jnp.where(core == 0, chunk, n - 1 - chunk)
        sums = (ahead < n - 1) & (ahead < t - 1)
        table = numbers(chunk, sums, 1 - core)
        grads = st["their_grads" if side else "grads"]
        st["sent"], st["share"] = hop(table, grads, st["weight"], st["line", t - 1, side])

    def offers_of(step):
        if step == 0:
            return [[st["tokens"]], [st["their_tokens"]]]
        kinds = kinds_of[step]
        return [
            [st["line", t, s] if mine else st["shared", t, 1 - s] for t, mine in kinds]
            for s in range(2)
        ]

    def piece_of(step, extra=()):
        table = numbers(choice_of[step], core)
        both = st["grads"], st["their_grads"]
        st["mix", step], *st["kept"] = piece(table, *offers_of(step), *both, extra)

    def sum_of(step):
        at = (2 * chunk_of[step] + core)[None]
        pair = st.pop(("mix", step)), st.pop(("x", step))
        shape = n * width, width
        st["wg"], st["ours", step] = place_sum(at, *pair, st.get("wg"), shape, width // 2)

    def place_of(step, theirs):
        at = (2 * chunk_of[step] + 1 - core)[None]
        st["wg"] = place(at, theirs, st["wg"], (n * width, width))

    st["weight"], st["tokens"], st["z"] = weight, tokens, z
    line = along(tokens)
    st["their_tokens"] = other_core(tokens)
    theirs = other_core(cotangent)
    mine = jnp.stack([jnp.swapaxes(down_maps, 1, 2), up_maps]).reshape(2, -1, width)
    st["fetched"] = other_tenant(lax.dynamic_index_in_dim(mine, core, 0, keepdims=False))
    st["mine"] = mine
    blocks = rows // BLOCK_ROWS
    first = (owner * 2 + core) * blocks
    their_first = (owner * 2 + 1 - core) * blocks
    places = numbers(first, their_first, (2 - owner) * held)
    table = jnp.concatenate([counts, slot_of, places])
    st["grads"], st["their_grads"], st["relative"], st["live"] = masked(
        table, counts.shape[0], slots, cotangent, theirs
    )
    fence()

    coming = along(st["their_tokens"])
    piece_of(0)
    swapped = other_tenant(st["mix", 0])
    shared = other_core(st["fetched"])
    names = ("relative", "tokens", "grads")
    st["down"], st["up"], st["part"] = ranks_of(
        core[None], rank, st.pop("mine"), st.pop("fetched"), shared, *[st[v] for v in names]
    )
    st["line", 1, 0] = line
    line = coming
    fence()

    wg_share = None
    for k in range(2, 2 * n + 1):
        t, side, step = k // 2 + 1, k % 2, k // 2
        last = k == 2 * n
        if not last:
            hop_of(k)
        if k == 2:
            for d in range(1, n):
                pairs = [(i, (i + d) % n) for i in range(n)]
                st["part", d] = lax.ppermute(st["part"], "tensor", pairs)
        if k == 3:
            st["x", 0] = swapped
            st["came"] = other_core(st.pop("for_sibling"))
        if k == 6:
            st["maps_x"] = other_tenant(st["kept"].pop())
        fence()
        if k == 6:
            swapped = other_tenant(st["mix", 2])
        if not last:
            coming = along(st.pop("sent"))
            st["shared", t - 1, side] = other_core(st.pop("share"))
        if side == 1:
            extra = ()
            if step == 2:
                extra = st.pop("maps"), st.pop("came")
            if step == n - 1:
                kept = st.pop("kept")
            piece_of(step, extra)
            if step == n - 1:
                st["kept"] = kept[:1]
            if step > 1:
                st["x", step - 1] = swapped
            fence()
            if step != 2:
                swapped = other_tenant(st["mix", step])
        elif k >= 4:
            sum_of(step - 2)
        if side == 0 and 4 <= k < 2 * n:
            wg_share = other_core(st["ours", step - 2])
        if k >= 6 and side == 0:
            place_of(step - 3, st.pop("theirs"))
        if k == 2:
            st["low"], st["back"], st["maps"], st["for_sibling"] = maps_of(
                core[None],
                rank,
                slots,
                [st.pop("part")] + [st.pop(("part", d)) for d in range(1, n)],
                *[st[v] for v in names],
            )
        if k == 4:
            st["term"] = term_of(st["z"][None], st["grads"], st["weight"])
        if k == 6:
            maps = [st.pop(v) for v in ("low", "up", "back", "down")]
            st["lora_out"], st["lora_in"] = lora_of(*maps)
        if last:
            offers = [offers_of(s) for s in range(n)]
            table = numbers(core, *chunk_of, *choice_of)
            st["query_here"], *st["query_there"] = query_parts(table, offers, st["weight"])
        st["line", (k - 1) // 2 + 1, 1 - side] = line
        line = coming
        if side == 1 and wg_share is not None:
            st["theirs"] = wg_share
            wg_share = None
        fence()

    kept = st.pop("kept")[0] + st.pop("maps_x").astype(F32)
    other = other_core(kept)
    there = [other_core(v) for v in st.pop("query_there")]
    theirs = [other_core(v) for v in jnp.split(st["line", n, 1], 2)]
    sums = [st.pop(v) for v in ("query_here", "live", "lora_out", "term", "lora_in")]
    ends = st["line", n, 0]
    done = finish(core, *sums, ends, *there, *theirs, kept, other)
    st["query"], st["token_grad"], down_grad, up_grad = done
    st["down_grad"] = jnp.swapaxes(down_grad.reshape(held, rank, width), 1, 2)
    st["up_grad"] = up_grad.reshape(held, rank, width)
    fence()
    st["x", n - 1] = swapped
    fence()
    st["ours", n - 1] = add(st["mix", n - 1], st["x", n - 1])
    earlier = other_core(st["ours", n - 2])
    theirs = other_core(st["ours", n - 1])
    shape = n * width, width
    mine_at = (2 * chunk_of[n - 1] + core)[None]
    st["wg"] = place(mine_at, st["ours", n - 1], st["wg"], shape)
    place_of(n - 2, earlier)
    place_of(n - 1, theirs)
    return st["query"], st["token_grad"], st["wg"], st["down_grad"], st["up_grad"]


def solution(mesh):
    placed = (
        P(("groups", "tenant", "dp"), "tensor"),
        P(None, "tensor"),
        P("tenant", "tensor", None),
        P("tenant", None, "tensor"),
        P("groups"),
        P(),
        P(("groups", "tenant", "dp"), "tensor"),
    )
    short = mesh.shape["tensor"] == 4
    paired = mesh.shape["tenant"] == 2 and mesh.shape["dp"] == 2
    return jax.shard_map(
        shards_line if short and paired else shards_general,
        mesh=mesh,
        in_specs=placed,
        out_specs=(
            P(("groups", "tenant", "dp"), "tensor"),
            P(("groups", "tenant", "dp"), "tensor"),
            P("groups", "tensor"),
            P(("groups", "tenant"), "tensor", None),
            P(("groups", "tenant"), None, "tensor"),
        ),
        check_vma=False,
    )
```

```python
import functools

import jax
import jax.numpy as jnp
from jax import lax
from jax.experimental import pallas as pl
from jax.experimental.pallas import tpu as pltpu
from jax.sharding import PartitionSpec as P

BLOCK_ROWS = 128
SCALE = 2.0
F32 = jnp.float32
B16 = jnp.bfloat16


def dot(a, b, ca, cb):
    return lax.dot_general(a, b, (((ca,), (cb,)), ((), ())), preferred_element_type=F32)


def lookup(source, position):
    match_mask = position[..., None] == jnp.arange(source.shape[0], dtype=jnp.int32)
    return jnp.sum(jnp.where(match_mask, source, 0), axis=-1)


def layout(tenant_row_counts, row_ids):
    block_count = (tenant_row_counts + BLOCK_ROWS - 1) // BLOCK_ROWS
    segment_offset = jnp.cumsum(block_count) - block_count
    block_ids = row_ids // BLOCK_ROWS
    tenant_of = (
        jnp.sum((segment_offset[None, :] <= block_ids[:, None]).astype(jnp.int32), axis=1) - 1
    )
    offset = row_ids - BLOCK_ROWS * lookup(segment_offset, tenant_of)
    return tenant_of, offset < lookup(tenant_row_counts, tenant_of)


def rank_partials(maps, rows, mask, slots):
    every = dot(maps, rows, 1, 1)
    every = every.reshape(slots, -1, rows.shape[0])
    return jnp.sum(jnp.where(mask[:, None, :], every, 0.0), axis=0)


def spread(values, mask):
    wide = jnp.where(mask[:, None, :], values[None], jnp.zeros((), values.dtype))
    return wide.reshape(-1, values.shape[-1])


def shards_general(tokens, weight, down_maps, up_maps, counts, slot_of, cotangent):
    rows, width = tokens.shape
    held, _, rank = down_maps.shape
    slots = held * lax.axis_size("tenant")
    owner = lax.axis_index("tenant")
    row_ids = lax.axis_index(("tenant", "dp")) * rows + jnp.arange(rows, dtype=jnp.int32)
    tenant, live = layout(counts, row_ids)
    slot = lookup(slot_of, tenant)
    mask = slot[None, :] == jnp.arange(slots, dtype=jnp.int32)[:, None]
    grads = jnp.where(live[:, None], cotangent, jnp.zeros_like(cotangent))
    kept = jnp.where(live[:, None], tokens, jnp.zeros_like(tokens))
    down = lax.all_gather(jnp.swapaxes(down_maps, 1, 2), "tenant", axis=0, tiled=True)
    up = lax.all_gather(up_maps, "tenant", axis=0, tiled=True)
    down, up = down.reshape(-1, width), up.reshape(-1, width)
    gathered = lax.all_gather(kept, "tensor", axis=1, tiled=True)
    part = jnp.stack(
        [rank_partials(down, kept, mask, slots), rank_partials(up, grads, mask, slots)]
    )
    low, back = lax.psum(part.astype(B16), "tensor")
    low, back = spread(low, mask), spread(back, mask)
    base = dot(gathered, weight, 1, 0)
    query = (base + (SCALE * dot(low, up, 0, 0)).astype(B16).astype(F32)).astype(B16)
    term = dot(grads, weight, 1, 1).astype(B16)
    summed = lax.psum_scatter(term, "tensor", scatter_dimension=1, tiled=True).astype(F32)
    lora = (SCALE * dot(back, down, 0, 0)).astype(B16).astype(F32)
    token_grad = jnp.where(live[:, None], summed + lora, 0.0).astype(B16)
    axes = ("tenant", "dp")
    weight_grad = lax.psum(dot(gathered, grads, 0, 0).astype(B16), axes)
    maps = jnp.stack([SCALE * dot(back, kept, 1, 0), SCALE * dot(low, grads, 1, 0)])
    maps = lax.psum(maps.astype(B16), axes).astype(F32).reshape(2, slots, rank, width)
    maps = lax.dynamic_slice_in_dim(maps, owner * held, held, 1)
    return query, token_grad, weight_grad, jnp.swapaxes(maps[0], 1, 2), maps[1]


def arrival_plan(n):
    plan = [[] for _ in range(n - 1)]
    for z in range(n):
        seen = []
        for t in range(1, n):
            if z - t >= 0:
                seen.append((t, 0, z - t))
            if z + t < n:
                seen.append((t, 1, z + t))
        for step, entry in enumerate(seen):
            plan[step].append(entry)
    return plan


def whole(array):
    return pl.BlockSpec(array.shape, lambda *_: (0,) * array.ndim)


def call(body, table, grid, arrays, specs, outs, out_specs, scratch, flops, aliases=None, pinned=(), limit=48):
    arrays = list(arrays)
    for at in pinned:
        arrays[at] = pltpu.with_memory_space_constraint(arrays[at], pltpu.HBM)
    return pl.pallas_call(
        body,
        grid_spec=pltpu.PrefetchScalarGridSpec(
            num_scalar_prefetch=1,
            grid=grid,
            in_specs=specs,
            out_specs=out_specs,
            scratch_shapes=scratch,
        ),
        out_shape=outs,
        input_output_aliases=aliases or {},
        compiler_params=pltpu.CompilerParams(vmem_limit_bytes=limit * 1024 * 1024),
        cost_estimate=pl.CostEstimate(flops=1, bytes_accessed=1, transcendentals=0),
    )(table, *arrays)


FREE = ()
HOP_STEPS = 2


def hop_body(table, grads, weight, came, goes, share):
    @pl.when(pl.program_id(0) == table[2])
    def _():
        share[...] = came[...]

    @pl.when(table[1] == 0)
    def _():
        goes[...] = came[...]

    @pl.when(table[1] != 0)
    def _():
        term = dot(grads[...], weight[...], 1, 1)
        goes[...] = (term + came[...].astype(F32)).astype(B16)


def hop(table, grads, weight, came):
    rows, width = came.shape
    half, step = width // 2, width // HOP_STEPS
    cols = pl.BlockSpec((rows, step), lambda j, t: (0, j))
    return call(
        hop_body,
        table,
        (HOP_STEPS,),
        [grads, weight, came],
        [
            whole(grads),
            pl.BlockSpec((step, width), lambda j, t: (HOP_STEPS * t[0] + j, 0)),
            cols,
        ],
        [jax.ShapeDtypeStruct((rows, width), B16), jax.ShapeDtypeStruct((rows, half), B16)],
        [cols, pl.BlockSpec((rows, half), lambda j, t: (0, 0))],
        [],
        0,
    )


def start_chosen(choice, offers, core, target, done):
    rows, half = target.shape
    for at, offer in enumerate(offers):

        @pl.when(choice == at)
        def _(offer=offer):
            source = offer
            if offer.shape[1] != half:
                source = offer.at[:, pl.ds(pl.multiple_of(core * half, half), half)]
            pltpu.make_async_copy(source, target, done).start()


def wait_chosen(target, done):
    pltpu.make_async_copy(target, target, done).wait()


def piece_body(count, extra, table, *refs):
    ours, theirs = refs[:count], refs[count : 2 * count]
    grads, their_grads = refs[2 * count : 2 * count + 2]
    rest = refs[2 * count + 2 :]
    out, a, b, done = rest[2 * extra], *rest[-3:]
    half = a.shape[1]

    @pl.when(pl.program_id(0) == 0)
    def _():
        start_chosen(table[0], ours, table[1], a, done.at[0])
        start_chosen(table[0], theirs, table[1], b, done.at[1])
        wait_chosen(a, done.at[0])
        wait_chosen(b, done.at[1])

    mix = dot(a[...], grads[...], 0, 0) + dot(b[...], their_grads[...], 0, 0)
    out[...] = mix.astype(B16)
    if extra:
        maps, came, kept, sent = rest[0], rest[1], rest[3], rest[4]
        split = kept.shape[0]
        total = maps[...] + came[...].astype(F32)
        kept[...] = total[:split]
        sent[...] = total[split:].astype(B16)


def piece(table, ours, theirs, grads, their_grads, extra=()):
    rows, width = grads.shape
    half = width // 2

    def cols(count):
        return pl.BlockSpec((count, width // 2), lambda j, t: (0, j))

    split = extra[0].shape[0] // 2 if extra else 0
    outs = [jax.ShapeDtypeStruct((half, width), B16)]
    if extra:
        outs.append(jax.ShapeDtypeStruct((split, width), F32))
        outs.append(jax.ShapeDtypeStruct((split, width), B16))
    return call(
        functools.partial(piece_body, len(ours), 1 if extra else 0),
        table,
        (2,),
        [*ours, *theirs, grads, their_grads, *extra],
        [pl.BlockSpec(memory_space=pltpu.HBM)] * (2 * len(ours))
        + [cols(rows), cols(rows)]
        + [cols(2 * split)] * len(extra),
        outs,
        [cols(v.shape[0]) for v in outs],
        [pltpu.VMEM((rows, half), B16)] * 2 + [pltpu.SemaphoreType.DMA((2,))],
        0,
        pinned=range(2 * len(ours)),
    )


def query_body(groups, n, half, table, *refs):
    offers, blocks = refs[: -6 - n], refs[-6 - n : -6]
    own_out, other_out, other_end, rows_in, weight_in, done = refs[-6:]
    rows = own_out.shape[0]

    @pl.when(pl.program_id(0) == 0)
    def _():
        at = 0
        waits = []
        for step, count in enumerate(groups):
            start = pl.multiple_of(table[1 + step] * half, half)
            for side in range(2):
                here = offers[at : at + count]
                at += count
                target = rows_in.at[pl.ds(side * rows, rows), pl.ds(start, half)]
                sem = done.at[2 * step + side]
                start_chosen(table[1 + n + step], here, table[0], target, sem)
                waits.append((target, sem))
        for target, sem in waits:
            wait_chosen(target, sem)

    for chunk in range(n):
        weight_in[pl.ds(chunk * half, half), :] = blocks[chunk][...]
    own_out[...] = dot(rows_in[pl.ds(0, rows), :], weight_in[...], 1, 0)
    other = dot(rows_in[pl.ds(rows, rows), :], weight_in[...], 1, 0).astype(B16)
    other_out[...] = other[: rows // 2]
    other_end[...] = other[rows // 2 :]


def query_parts(table, offers, weight):
    n = len(offers)
    rows, width = offers[0][0][0].shape[0], weight.shape[1]
    half = cols = width // 2
    flat = [v for pair in offers for side in pair for v in side]

    def block(chunk):
        return pl.BlockSpec((half, cols), lambda j, t: (2 * chunk + t[0], j))

    out = pl.BlockSpec((rows, cols), lambda j, t: (0, j))
    part = pl.BlockSpec((rows // 2, cols), lambda j, t: (0, j))
    return call(
        functools.partial(query_body, [len(pair[0]) for pair in offers], n, half),
        table,
        (2,),
        [*flat] + [weight] * n,
        [pl.BlockSpec(memory_space=pltpu.HBM)] * len(flat) + [block(c) for c in range(n)],
        [
            kept_in_hbm(jax.ShapeDtypeStruct((rows, width), F32)),
            jax.ShapeDtypeStruct((rows // 2, width), B16),
            jax.ShapeDtypeStruct((rows // 2, width), B16),
        ],
        [out, part, part],
        [
            pltpu.VMEM((2 * rows, n * half), B16),
            pltpu.VMEM((n * half, cols), B16),
            pltpu.SemaphoreType.DMA((2 * n,)),
        ],
        0,
        pinned=range(len(flat)),
        limit=28,
    )


def term_body(table, grads, weight, out):
    out[...] = dot(grads[...], weight[...], 1, 1).astype(B16)


def term_of(table, grads, weight):
    rows, width = grads.shape
    half = width // 2
    return call(
        term_body,
        table,
        (2,),
        [grads, weight],
        [whole(grads), pl.BlockSpec((half, width), lambda j, t: (2 * t[0] + j, 0))],
        kept_in_hbm(jax.ShapeDtypeStruct((rows, width), B16)),
        pl.BlockSpec((rows, half), lambda j, t: (0, j)),
        [],
        2 * rows * width * width,
    )


def into_target(value, target, shape, at, body, extra, outs, steps):
    rows, width = shape[2], shape[1]
    block = rows // steps
    spec = pl.BlockSpec((block, width), lambda i, t: (i, 0))
    arrays, specs, aliases = [value, *extra], [spec] * (1 + len(extra)), {}
    if target is not None:
        aliases = {1 + len(arrays): 0}
        arrays.append(target)
        specs.append(pl.BlockSpec(memory_space=pl.ANY))
    where = pl.BlockSpec((block, width), lambda i, t: (steps * t[0] + i, 0))
    return call(
        body,
        at,
        (steps,),
        arrays,
        specs,
        [jax.ShapeDtypeStruct(shape[:2], B16)] + [jax.ShapeDtypeStruct((rows, width), B16)] * outs,
        [where] + [spec] * outs,
        [],
        0,
        aliases,
    )


def place_body(table, value, *refs):
    refs[-1][...] = value[...]


def place(at, value, target, shape):
    return into_target(value, target, (*shape, value.shape[0]), at, place_body, (), 0, 2)[0]


def sum_body(table, a, b, *refs):
    total = (a[...].astype(F32) + b[...].astype(F32)).astype(B16)
    refs[-2][...] = total
    refs[-1][...] = total


def place_sum(at, a, b, target, shape, rows):
    return into_target(a, target, (*shape, rows), at, sum_body, (b,), 1, 2)


def ranks_body(rank, table, mine, fetched, shared, relative, tokens, grads, down, up, part):
    split = mine.shape[1]
    down[pl.ds(0, split), :] = mine[0]
    up[pl.ds(0, split), :] = mine[1]

    @pl.when(table[0] == 0)
    def _():
        down[pl.ds(split, split), :] = fetched[...]
        up[pl.ds(split, split), :] = shared[...]

    @pl.when(table[0] != 0)
    def _():
        down[pl.ds(split, split), :] = shared[...]
        up[pl.ds(split, split), :] = fetched[...]

    for kind, (maps, rows) in enumerate(((down, tokens), (up, grads))):
        every = dot(maps[...], rows[...], 1, 1)
        total = None
        for slot in range(2 * split // rank):
            own = jnp.where(relative[...] == slot, every[slot * rank : (slot + 1) * rank], 0.0)
            total = own if total is None else total + own
        part[pl.ds(kind * rank, rank), :] = total.astype(B16)


def ranks_of(table, rank, mine, fetched, shared, relative, tokens, grads):
    rows, width = tokens.shape
    arrays = [mine, fetched, shared, relative, tokens, grads]
    outs = [
        jax.ShapeDtypeStruct((2 * mine.shape[1], width), B16),
        jax.ShapeDtypeStruct((2 * mine.shape[1], width), B16),
        jax.ShapeDtypeStruct((2 * rank, rows), B16),
    ]
    body = functools.partial(ranks_body, rank)
    specs = [whole(v) for v in arrays]
    return call(body, table, (1,), arrays, specs, [kept_in_hbm(v) for v in outs], [whole(v) for v in outs], [], 0, pinned=(4,))


def maps_body(rank, count, table, *refs):
    relative, tokens, grads, low, back, kept, sent = refs[count:]
    total = refs[0][...].astype(F32)
    for part in refs[1:count]:
        total += part[...].astype(F32)
    total = total.astype(B16).astype(F32)
    for kind, wide in enumerate((low, back)):
        own = total[kind * rank : (kind + 1) * rank]
        for slot in range(wide.shape[0] // rank):
            spread_out = jnp.where(relative[...] == slot, own, 0.0)
            wide[pl.ds(slot * rank, rank), :] = spread_out.astype(B16)
    for kind, (wide, rows) in enumerate(((back, tokens), (low, grads))):
        term = SCALE * dot(wide[...], rows[...], 1, 0)

        @pl.when(table[0] == kind)
        def _(term=term):
            kept[...] = term

        @pl.when(table[0] != kind)
        def _(term=term):
            sent[...] = term.astype(B16)


def maps_of(table, rank, slots, parts, relative, tokens, grads):
    rows, width = tokens.shape
    arrays = [*parts, relative, tokens, grads]
    outs = [
        jax.ShapeDtypeStruct((slots * rank, rows), B16),
        jax.ShapeDtypeStruct((slots * rank, rows), B16),
        jax.ShapeDtypeStruct((slots * rank, width), F32),
        jax.ShapeDtypeStruct((slots * rank, width), B16),
    ]
    body = functools.partial(maps_body, rank, len(parts))
    specs = [whole(v) for v in arrays]
    return call(body, table, (1,), arrays, specs, [kept_in_hbm(v) for v in outs], [whole(v) for v in outs], [], 0, pinned=(len(parts) + 1,))


def lora_body(table, low, up, back, down, out, into):
    out[...] = (SCALE * dot(low[...], up[...], 0, 0)).astype(B16)
    into[...] = (SCALE * dot(back[...], down[...], 0, 0)).astype(B16)


def lora_of(low, up, back, down):
    rows, width = low.shape[1], up.shape[1]
    arrays = [low, up, back, down]
    out = jax.ShapeDtypeStruct((rows, width), B16)
    specs = [whole(v) for v in arrays]
    table = jnp.zeros((1,), jnp.int32)
    return call(lora_body, table, (1,), arrays, specs, [kept_in_hbm(out)] * 2, [whole(out)] * 2, [], 0)


def finish_body(table, here, live, out_lora, term, in_lora, ends, there, there_end, theirs, theirs_end, kept, other, query, token_grad, down, up):
    for i, (mine, sums) in enumerate(((there, theirs), (there_end, theirs_end))):

        @pl.when(pl.program_id(0) == i)
        def _(mine=mine, sums=sums):
            total = here[...] + mine[...].astype(F32) + out_lora[...].astype(F32)
            query[...] = jnp.where(live[...] > 0, total, 0.0).astype(B16)
            total = term[...].astype(F32) + in_lora[...].astype(F32) + ends[...].astype(F32)
            token_grad[...] = (total + sums[...].astype(F32)).astype(B16)

    @pl.when((pl.program_id(0) == 0) & (table[0] == 0))
    def _():
        down[...] = kept[...]
        up[...] = other[...]

    @pl.when((pl.program_id(0) == 0) & (table[0] != 0))
    def _():
        down[...] = other[...]
        up[...] = kept[...]


def finish(core, here, live, out_lora, term, in_lora, ends, *rest):
    rows, width = here.shape
    kept = rest[-1]
    spec = pl.BlockSpec((rows // 2, width), lambda i, t: (i, 0))
    thin = pl.BlockSpec((rows // 2, 1), lambda i, t: (i, 0))
    out = jax.ShapeDtypeStruct((rows, width), B16)
    small = jax.ShapeDtypeStruct(kept.shape, F32)
    return call(
        finish_body,
        core[None],
        (2,),
        [here, live, out_lora, term, in_lora, ends, *rest],
        [spec, thin, spec, spec, spec, spec] + [whole(v) for v in rest],
        [out, out, small, small],
        [spec, spec, whole(small), whole(small)],
        [],
        0,
    )


def add_body(table, a, b, out):
    out[...] = (a[...].astype(F32) + b[...].astype(F32)).astype(B16)


def add(a, b):
    rows, width = a.shape
    spec = pl.BlockSpec((rows // 2, width), lambda i, t: (i, 0))
    out = jax.ShapeDtypeStruct(a.shape, B16)
    table = jnp.zeros((1,), jnp.int32)
    return call(add_body, table, (2,), [a, b], [spec] * 2, out, spec, [], 0, pinned=(0, 1))


def mask_body(tenants, slots, table, mine, theirs, grads, their_grads, slot_rows, live):
    blocks = mine.shape[0] // BLOCK_ROWS
    row = lax.broadcasted_iota(jnp.int32, (BLOCK_ROWS, 1), 0)
    for side, (rows_in, rows_out) in enumerate(((mine, grads), (theirs, their_grads))):
        for b in range(blocks):
            block = table[2 * tenants + side] + b
            start = jnp.int32(0)
            left = slot = jnp.int32(0)
            for t in range(tenants):
                here = start <= block
                left = jnp.where(here, table[t] - BLOCK_ROWS * (block - start), left)
                slot = jnp.where(here, table[tenants + t], slot)
                start = start + (table[t] + BLOCK_ROWS - 1) // BLOCK_ROWS
            at = pl.ds(b * BLOCK_ROWS, BLOCK_ROWS)
            alive = row < left
            rows_out[at, :] = jnp.where(alive, rows_in[at, :].astype(F32), 0.0).astype(B16)
            if side == 0:
                live[at, :] = jnp.where(alive, 1.0, 0.0)
                placed = lax.rem(slot + table[2 * tenants + 2], slots)
                slot_rows[:, at] = jnp.full((1, BLOCK_ROWS), placed, jnp.int32)


def masked(table, tenants, slots, mine, theirs):
    rows, width = mine.shape
    outs = [
        jax.ShapeDtypeStruct((rows, width), B16),
        jax.ShapeDtypeStruct((rows, width), B16),
        jax.ShapeDtypeStruct((1, rows), jnp.int32),
        jax.ShapeDtypeStruct((rows, 1), F32),
    ]
    body = functools.partial(mask_body, tenants, slots)
    specs = [whole(mine), whole(theirs)]
    return call(body, table, (1,), [mine, theirs], specs, [*outs[:3], kept_in_hbm(outs[3])], [whole(v) for v in outs], [], 0, pinned=(0, 1))


def kept_in_hbm(shape):
    return pltpu.HBM(shape.shape, shape.dtype)


def shards_line(tokens, weight, down_maps, up_maps, counts, slot_of, cotangent):
    rows, width = tokens.shape
    held, _, rank = down_maps.shape
    n = lax.axis_size("tensor")
    slots = held * 2
    z = lax.axis_index("tensor")
    owner = lax.axis_index("tenant")
    core = lax.axis_index("dp")
    swap = [(0, 1), (1, 0)]
    ahead = jnp.where(core == 0, z, n - 1 - z)
    line_pairs = []
    for i in range(n - 1):
        line_pairs += [(2 * i, 2 * i + 2), (2 * i + 3, 2 * i + 1)]

    def along(value):
        return lax.ppermute(value, ("tensor", "dp"), line_pairs)

    def other_tenant(value):
        return lax.ppermute(value, "tenant", swap)

    def other_core(value):
        return lax.ppermute(value, "dp", swap)

    def numbers(*values):
        return jnp.stack([v.astype(jnp.int32) for v in values])

    chunk_of = [z]
    choice_of = [jnp.zeros((), jnp.int32)]
    kinds_of = [None]
    for choices in arrival_plan(n):
        kinds = sorted({(t, d == c) for t, d, _ in choices for c in range(2)})
        chunk = choice = jnp.zeros((), jnp.int32)
        for at, (t, direction, source) in enumerate(choices):
            chunk = jnp.where(z == at, source, chunk)
            for c in range(2):
                here = (z == at) & (core == c)
                choice = jnp.where(here, kinds.index((t, direction == c)), choice)
        chunk_of.append(chunk)
        choice_of.append(choice)
        kinds_of.append(kinds)

    st = {}

    def fence():
        names = [name for name in st if name not in FREE]
        st.update(zip(names, lax.optimization_barrier([st[name] for name in names])))

    def hop_of(k):
        t, side = k // 2 + 1, k % 2
        chunk = jnp.clip(n + ahead + 1 - t, 0, n - 1)
        chunk = jnp.where(core == 0, chunk, n - 1 - chunk)
        sums = (ahead < n - 1) & (ahead < t - 1)
        table = numbers(chunk, sums, 1 - core)
        grads = st["their_grads" if side else "grads"]
        st["sent"], st["share"] = hop(table, grads, st["weight"], st["line", t - 1, side])

    def offers_of(step):
        if step == 0:
            return [[st["tokens"]], [st["their_tokens"]]]
        kinds = kinds_of[step]
        return [
            [st["line", t, s] if mine else st["shared", t, 1 - s] for t, mine in kinds]
            for s in range(2)
        ]

    def piece_of(step, extra=()):
        table = numbers(choice_of[step], core)
        both = st["grads"], st["their_grads"]
        st["mix", step], *st["kept"] = piece(table, *offers_of(step), *both, extra)

    def sum_of(step):
        at = (2 * chunk_of[step] + core)[None]
        pair = st.pop(("mix", step)), st.pop(("x", step))
        shape = n * width, width
        st["wg"], st["ours", step] = place_sum(at, *pair, st.get("wg"), shape, width // 2)

    def place_of(step, theirs):
        at = (2 * chunk_of[step] + 1 - core)[None]
        st["wg"] = place(at, theirs, st["wg"], (n * width, width))

    st["weight"], st["tokens"], st["z"] = weight, tokens, z
    line = along(tokens)
    st["their_tokens"] = other_core(tokens)
    theirs = other_core(cotangent)
    mine = jnp.stack([jnp.swapaxes(down_maps, 1, 2), up_maps]).reshape(2, -1, width)
    st["fetched"] = other_tenant(lax.dynamic_index_in_dim(mine, core, 0, keepdims=False))
    st["mine"] = mine
    blocks = rows // BLOCK_ROWS
    first = (owner * 2 + core) * blocks
    their_first = (owner * 2 + 1 - core) * blocks
    places = numbers(first, their_first, (2 - owner) * held)
    table = jnp.concatenate([counts, slot_of, places])
    st["grads"], st["their_grads"], st["relative"], st["live"] = masked(
        table, counts.shape[0], slots, cotangent, theirs
    )
    fence()

    coming = along(st["their_tokens"])
    piece_of(0)
    swapped = other_tenant(st["mix", 0])
    shared = other_core(st["fetched"])
    names = ("relative", "tokens", "grads")
    st["down"], st["up"], st["part"] = ranks_of(
        core[None], rank, st.pop("mine"), st.pop("fetched"), shared, *[st[v] for v in names]
    )
    st["line", 1, 0] = line
    line = coming
    fence()

    wg_share = None
    for k in range(2, 2 * n + 1):
        t, side, step = k // 2 + 1, k % 2, k // 2
        last = k == 2 * n
        if not last:
            hop_of(k)
        if k == 2:
            for d in range(1, n):
                pairs = [(i, (i + d) % n) for i in range(n)]
                st["part", d] = lax.ppermute(st["part"], "tensor", pairs)
        if k == 3:
            st["x", 0] = swapped
            st["came"] = other_core(st.pop("for_sibling"))
        if k == 6:
            st["maps_x"] = other_tenant(st["kept"].pop())
        fence()
        if k == 6:
            swapped = other_tenant(st["mix", 2])
        if not last:
            coming = along(st.pop("sent"))
            st["shared", t - 1, side] = other_core(st.pop("share"))
        if side == 1:
            extra = ()
            if step == 2:
                extra = st.pop("maps"), st.pop("came")
            if step == n - 1:
                kept = st.pop("kept")
            piece_of(step, extra)
            if step == n - 1:
                st["kept"] = kept[:1]
            if step > 1:
                st["x", step - 1] = swapped
            fence()
            if step != 2:
                swapped = other_tenant(st["mix", step])
        elif k >= 4:
            sum_of(step - 2)
        if side == 0 and 4 <= k < 2 * n:
            wg_share = other_core(st["ours", step - 2])
        if k >= 6 and side == 0:
            place_of(step - 3, st.pop("theirs"))
        if k == 2:
            st["low"], st["back"], st["maps"], st["for_sibling"] = maps_of(
                core[None],
                rank,
                slots,
                [st.pop("part")] + [st.pop(("part", d)) for d in range(1, n)],
                *[st[v] for v in names],
            )
        if k == 4:
            st["term"] = term_of(st["z"][None], st["grads"], st["weight"])
        if k == 6:
            maps = [st.pop(v) for v in ("low", "up", "back", "down")]
            st["lora_out"], st["lora_in"] = lora_of(*maps)
        if last:
            offers = [offers_of(s) for s in range(n)]
            table = numbers(core, *chunk_of, *choice_of)
            st["query_here"], *st["query_there"] = query_parts(table, offers, st["weight"])
        st["line", (k - 1) // 2 + 1, 1 - side] = line
        line = coming
        if side == 1 and wg_share is not None:
            st["theirs"] = wg_share
            wg_share = None
        fence()

    kept = st.pop("kept")[0] + st.pop("maps_x").astype(F32)
    other = other_core(kept)
    there = [other_core(v) for v in st.pop("query_there")]
    theirs = [other_core(v) for v in jnp.split(st["line", n, 1], 2)]
    sums = [st.pop(v) for v in ("query_here", "live", "lora_out", "term", "lora_in")]
    ends = st["line", n, 0]
    done = finish(core, *sums, ends, *there, *theirs, kept, other)
    st["query"], st["token_grad"], down_grad, up_grad = done
    st["down_grad"] = jnp.swapaxes(down_grad.reshape(held, rank, width), 1, 2)
    st["up_grad"] = up_grad.reshape(held, rank, width)
    fence()
    st["x", n - 1] = swapped
    fence()
    st["ours", n - 1] = add(st["mix", n - 1], st["x", n - 1])
    earlier = other_core(st["ours", n - 2])
    theirs = other_core(st["ours", n - 1])
    shape = n * width, width
    mine_at = (2 * chunk_of[n - 1] + core)[None]
    st["wg"] = place(mine_at, st["ours", n - 1], st["wg"], shape)
    place_of(n - 2, earlier)
    place_of(n - 1, theirs)
    return st["query"], st["token_grad"], st["wg"], st["down_grad"], st["up_grad"]


def solution(mesh):
    placed = (
        P(("groups", "tenant", "dp"), "tensor"),
        P(None, "tensor"),
        P("tenant", "tensor", None),
        P("tenant", None, "tensor"),
        P("groups"),
        P(),
        P(("groups", "tenant", "dp"), "tensor"),
    )
    short = mesh.shape["tensor"] == 4
    paired = mesh.shape["tenant"] == 2 and mesh.shape["dp"] == 2
    return jax.shard_map(
        shards_line if short and paired else shards_general,
        mesh=mesh,
        in_specs=placed,
        out_specs=(
            P(("groups", "tenant", "dp"), "tensor"),
            P(("groups", "tenant", "dp"), "tensor"),
            P("groups", "tensor"),
            P(("groups", "tenant"), "tensor", None),
            P(("groups", "tenant"), None, "tensor"),
        ),
        check_vma=False,
    )
```
